256 devices in a mesh: dp: 16 (over y, x_hi, core), fsdp: 16 (over x_lo, z).
Axes of the slice: x: 4 (x_hi: 2, x_lo: 2; x = x_hi * 2 + x_lo), y: 4, z: 8, core: 2. Of those that a mesh axis runs over, the one named last changes fastest.
Arguments:
- grads: bfloat16 [16, 1024, 2, 16384], P('dp', 'fsdp'), may hold values from -0.119628906 to 0.119628906
- left_basis_t: bfloat16 [1024, 2, 16384], P('fsdp', None, 'dp'), may hold values from -0.1875 to 0.1875
- right_basis: bfloat16 [1024, 2, 16384], P('fsdp', None, 'dp'), may hold values from -0.1875 to 0.1875
- first_moment: float32 [1024, 2, 16384], P('fsdp', None, 'dp'), may hold values from -0.18 to 0.18
- second_moment: float32 [1024, 2, 16384], P('fsdp', None, 'dp'), may hold values from 0.001 to 0.01
- left_gram: float32 [1024, 2, 16384], P('fsdp', None, 'dp'), may hold values from -1.8 to 1.8
- right_gram: float32 [1024, 2, 16384], P('fsdp', None, 'dp'), may hold values from -1.8 to 1.8
Outputs:
- update: bfloat16 [1024, 2, 16384], P('fsdp')
- new_first: float32 [1024, 2, 16384], P('fsdp', None, 'dp')
- new_second: float32 [1024, 2, 16384], P('fsdp', None, 'dp')
- new_left_gram: float32 [1024, 2, 16384], P('fsdp', None, 'dp')
- new_right_gram: float32 [1024, 2, 16384], P('fsdp', None, 'dp')
The draws below stay inside these ranges and needn't reach their ends.
All inputs are finite; a program needn't handle non-finite values.
Results may differ from the reference program's by a relative error of at most 0.017.
Values may be sent and summed in bfloat16 or wider, within the bound.
A program may use at most 128 MiB of HBM per device.

```python
import math
import jax
import jax.numpy as jnp
from jax import lax

BLOCK = 1024
KB = 2
COLS = 16384
N_DP = 16


def spiked(entries, rng, source, target, shards_of, factor):
    def block_of(dim):
        return (jnp.arange(entries.shape[dim]) // (entries.shape[dim] // shards_of)).reshape((-1,) + (1,) * (entries.ndim - 1 - dim))

    near = jax.random.permutation(rng, shards_of)[block_of(target)]
    second = (block_of(target) + shards_of // 2) % shards_of
    return jnp.where((block_of(source) == near) | (block_of(source) == second), factor * entries, entries)


def level_of(own_key, shape, split, smallest, largest):
    factor_of, own = 1.0, jax.random.fold_in(own_key, 6)
    for axis_at, blocks in split:
        steps = jnp.exp(jax.random.uniform(jax.random.fold_in(own, axis_at), (blocks,), jnp.float32, smallest / len(split), largest / len(split)))
        factor_of = factor_of * jnp.repeat(steps, shape[axis_at] // blocks).reshape([-1 if axis == axis_at else 1 for axis in range(len(shape))])
    return factor_of


def gaussian(key, extent, width, reach, split=(), dtype=jnp.bfloat16):
    factor_of = level_of(key, extent, split, -0.22, 0.18) if split else 1.0
    result = jax.random.normal(key, extent, jnp.float32) * width * factor_of
    return jnp.minimum(jnp.maximum(result, -reach), reach).astype(dtype)


def gaussian_with(rng, shape, scale, reach, pieces, heavy, dtype=jnp.bfloat16):
    entries = scale * jax.random.normal(rng, shape, jnp.float32)
    if pieces:
        entries = entries * level_of(rng, shape, pieces, -0.22, 0.18)
    return jnp.clip(spiked(entries, jax.random.fold_in(rng, 3), *heavy), -reach, reach).astype(dtype)


def setup_inputs(seed: int = 0) -> dict:
    keys = jax.random.split(jax.random.key(seed), 8)
    return {
        "grads": gaussian_with(keys[0], (N_DP, BLOCK, KB, COLS), 0.02, 0.119628906, ((0, 16), (1, 16)), (0, 3, 16, 2.0)),
        "left_basis_t": gaussian(keys[1], (BLOCK, KB, COLS), BLOCK ** -0.5, 0.1875, ((0, 16), (2, 16))),
        "right_basis": gaussian(keys[2], (BLOCK, KB, COLS), BLOCK ** -0.5, 0.1875, ((0, 16), (2, 16))),
        "first_moment": gaussian(keys[3], (BLOCK, KB, COLS), 0.03, 0.18, ((0, 16), (2, 16)), jnp.float32),
        "second_moment": jnp.clip(jnp.exp(math.log(0.01) - 2.30258502 * jax.random.uniform(keys[4], (BLOCK, KB, COLS), jnp.float32) ** level_of(keys[4], (BLOCK, KB, COLS), ((0, 16), (2, 16)), -0.2, 0.2)), 0.001, 0.01),
        "left_gram": gaussian(keys[5], (BLOCK, KB, COLS), 0.3, 1.8, ((0, 16), (2, 16)), jnp.float32),
        "right_gram": gaussian(keys[6], (BLOCK, KB, COLS), 0.3, 1.8, ((0, 16), (2, 16)), jnp.float32),
    }


def split_blocks(array):
    shaped = array.reshape(array.shape[0], KB, N_DP, BLOCK)
    return jnp.moveaxis(shaped, 2, 0)

def merge_blocks(array):
    return jnp.moveaxis(array, 0, 2).reshape(BLOCK, KB, N_DP * BLOCK)

def one_block(block_parts):
    grad_block, left_t, right_q, moment_one, moment_two, gram_left, gram_right = block_parts
    grad_wide = grad_block.astype(jnp.float32)
    left_new = 0.95 * gram_left + 0.05 * jnp.einsum('ibc,rbc->ibr', grad_wide, grad_wide)
    right_new = 0.95 * gram_right + 0.05 * jnp.einsum('rbi,rbc->ibc', grad_wide, grad_wide)
    left_wide = left_t.astype(jnp.float32)
    right_expanded = right_q.astype(jnp.float32)
    partial_rotation_step = jnp.einsum('ebr,rbc->ebc', left_wide, grad_wide).astype(jnp.bfloat16)
    eigen_rotated_grad = jnp.einsum('tnj,jny->tny', partial_rotation_step.astype(jnp.float32), right_expanded)
    first_new = 0.9 * moment_one + 0.1 * eigen_rotated_grad
    second_new = 0.95 * moment_two + 0.05 * eigen_rotated_grad * eigen_rotated_grad
    normalized_update = (first_new / (jnp.sqrt(second_new) + 1e-08)).astype(jnp.bfloat16)
    projected_blocks = jnp.einsum('pvd,nvd->pvn', normalized_update.astype(jnp.float32), right_expanded).astype(jnp.bfloat16)
    update_block = jnp.einsum('ebr,ebc->rbc', left_wide, projected_blocks.astype(jnp.float32)).astype(jnp.bfloat16)
    return (update_block, first_new, second_new, left_new, right_new)

def reference(grads, left_basis_t, right_basis, first_moment, second_moment, left_gram, right_gram):
    summed = lax.optimization_barrier(jnp.sum(grads.astype(jnp.float32), axis=0)).astype(jnp.bfloat16)
    block_parts = (split_blocks(summed), split_blocks(left_basis_t), split_blocks(right_basis), split_blocks(first_moment), split_blocks(second_moment), split_blocks(left_gram), split_blocks(right_gram))
    results = lax.map(one_block, block_parts)
    update, new_first, new_second, new_left, fresh_right_factor = results
    return (merge_blocks(update), merge_blocks(new_first), merge_blocks(new_second), merge_blocks(new_left), merge_blocks(fresh_right_factor))
```

```python
import jax
import jax.numpy as jnp
from jax import lax
from jax.experimental import pallas as pl
from jax.experimental.pallas import tpu as pltpu
from jax.sharding import PartitionSpec as P

MESH = pl.DeviceIdType.MESH
F32, BF16 = jnp.float32, jnp.bfloat16
NCOPY = 200
H = 2
W = 1024 // H
PIECE = 1024 // H
CONTRACT_LAST = (((1,), (1,)), ((), ()))


def rows_view(x):
    i, b, n = x.shape
    return x.reshape(i, b, n // 128, 128).transpose(0, 2, 1, 3)


class Peers:
    def __init__(self):
        dp, fs = lax.axis_index("dp"), lax.axis_index("fsdp")
        self.y, self.xh, self.c = lax.div(dp, 4), lax.rem(lax.div(dp, 2), 2), lax.rem(dp, 2)
        self.xl, self.z = lax.div(fs, 8), lax.rem(fs, 8)

    def at(self, dy=0, dxh=0, dc=0, dxl=0, dz=0):
        y, xh, c = lax.rem(self.y + dy, 4), lax.rem(self.xh + dxh, 2), lax.rem(self.c + dc, 2)
        xl, z = lax.rem(self.xl + dxl, 2), lax.rem(self.z + dz, 8)
        return ((y * 2 + xh) * 2 + c, xl * 8 + z)


def kernel(
    g, lt, qr, m1, m2,
    out, rot, pleft, pright,
    in_bf, mom_in, own, other, summed, y_recv, x_send, x_recv, acc,
    q_split, q_full, l_split, l_rows, l_perm, l_all, l_t,
    g_full, mom, mom_recv, y_rot, n_buf, m_full, r_buf, r_recv, pl_buf, pl_recv, pr_buf, pr_recv,
    g_cols, up_send, up_recv, pack, up_piece,
    ss, rs, ls,
):
    k = Peers()
    y, xh, c, xl, z = k.y, k.xh, k.c, k.xl, k.z
    count = [0, 0]
    unsent = []

    def remote(src, dst, peer):
        n = count[0]
        count[0] += 1
        copy = pltpu.make_async_remote_copy(
            src, dst, ss.at[n], rs.at[n], device_id=peer, device_id_type=MESH
        )
        unsent.append(copy)
        return copy

    def send(src, dst, peer):
        copy = remote(src, dst, peer)
        copy.start()
        return copy

    def local(src, dst):
        n = count[1]
        count[1] += 1
        copy = pltpu.make_async_copy(src, dst, ls.at[n])
        copy.start()
        return copy

    partners = (
        [k.at(dc=1), k.at(dxl=1), k.at(dxh=1), k.at(dxh=1, dxl=1)]
        + [k.at(dy=o) for o in (1, 2, 3)]
        + [k.at(dz=o) for o in range(1, 8)]
    )
    barrier = pltpu.get_barrier_semaphore()
    for peer in partners:
        pl.semaphore_signal(barrier, inc=1, device_id=peer, device_id_type=MESH)

    load_q = local(qr, in_bf.at[0])
    load_l = local(lt, in_bf.at[1])
    load_own = [local(g.at[pl.ds(q * 32, 32), :, c], own.at[q]) for q in range(2)]
    load_m = [local(m1, mom_in.at[0]), local(m2, mom_in.at[1])]

    def split_bf(src, dst):
        acc[...] = src[...].reshape(1024, 128).astype(F32)
        for b in range(2):
            for t in range(8):
                dst[b, :, pl.ds(t * 128, 128)] = acc[pl.ds(t * 2 + b, 64, stride=16), :].astype(BF16)

    class ZGather:
        def __init__(self, ref):
            self.ref, self.copies = ref, {}

        def start(self, s, j):
            for d in (1, -1):
                if s == 4 and j != (d == -1):
                    continue
                at = self.ref(lax.rem(xl + j, 2), lax.rem(z - d * (s - 1) + 8, 8))
                self.copies[s, j, d] = send(at, at, k.at(dz=d % 8))

        def arrive(self, s, j):
            for d in (1, -1):
                if (s, j, d) in self.copies:
                    self.copies[s, j, d].wait_recv()

        def step(self, s, j):
            self.arrive(s, j)
            if s < 4:
                self.start(s + 1, j)

    zq = ZGather(lambda j, zz: q_full.at[j, zz])
    zg = [
        ZGather(lambda j, zz, q=q: g_full.at[j, zz, pl.ds(q * 32, 32), :]) for q in range(2)
    ]
    zm = [ZGather(lambda j, zz, h=h: m_full.at[h, j, zz]) for h in range(H)]

    load_q.wait()
    split_bf(in_bf.at[0], q_split)
    q_full[xl, z] = q_split[xl]
    pl.semaphore_wait(barrier, len(partners))

    core = [send(g.at[pl.ds(q * 32, 32), :, 1 - c], other.at[q], k.at(dc=1)) for q in range(2)]
    xq = send(q_split.at[1 - xl], q_full.at[xl, z], k.at(dxl=1))
    zq.start(1, 0)
    load_l.wait()
    split_bf(in_bf.at[1], l_split)
    xt = send(l_split.at[1 - xl], l_rows.at[xl], k.at(dxl=1))
    l_rows[xl] = l_split[xl]

    y_copies = {}

    def core_sum(q):
        load_own[q].wait()
        core[q].wait_recv()
        for o in (2, 1, 3, 0):
            yy = lax.rem(y + o, 4)

            @pl.loop(0, 8)
            def _(i):
                at = (q, pl.ds(i * 4, 4), pl.ds(yy * 2, 2))
                total = own[at].astype(F32) + other[at].astype(F32)
                summed[q, yy, pl.ds(i * 4, 4)] = total.astype(BF16)

            if o:
                y_copies[q, o] = send(summed.at[q, yy], y_recv.at[q, o - 1], k.at(dy=o))

    x_copies = {}

    def y_sum(q):
        for o in (1, 2, 3):
            y_copies[q, o].wait_recv()

        @pl.loop(0, 8)
        def _(i):
            at = pl.ds(i * 4, 4)
            total = summed[q, y, at].astype(F32)
            for o in range(3):
                total += y_recv[q, o, at].astype(F32)
            acc[pl.ds(i * 128, 128), :] = total.reshape(128, 128)

        for e in range(2):
            for b in range(2):
                for t in range(8):
                    x_send[q, e, b, :, pl.ds(t * 128, 128)] = acc[
                        pl.ds(e * 16 + t * 2 + b, 32, stride=32), :
                    ].astype(BF16)
        for n, (dh, dl) in enumerate(((1, 1), (1, 0), (0, 1))):
            x_copies[q, n] = send(
                x_send.at[q, lax.rem(xh + dh, 2), lax.rem(xl + dl, 2)],
                x_recv.at[q, n],
                k.at(dxh=dh, dxl=dl),
            )

    def x_sum(q):
        at = pl.ds(q * 32, 32)
        x_copies[q, 1].wait_recv()
        g_full[xl, z, at] = (
            x_send[q, xh, xl].astype(F32) + x_recv[q, 1].astype(F32)
        ).astype(BF16)
        zg[q].start(1, 0)
        x_copies[q, 0].wait_recv()
        x_copies[q, 2].wait_recv()
        g_full[1 - xl, z, at] = (x_recv[q, 0].astype(F32) + x_recv[q, 2].astype(F32)).astype(BF16)
        zg[q].start(1, 1)

    core_sum(0)
    xq.wait_recv()
    zq.start(1, 1)
    zq.step(1, 0)
    core_sum(1)
    zq.step(1, 1)

    for n in range(2):
        load_m[n].wait()
        for b in range(2):
            for t in range(8):
                mom[n, b, :, pl.ds(t * 128, 128)] = mom_in[n, pl.ds(t * 2 + b, 64, stride=16), :]
    xm = send(mom.at[:, 1 - xl], mom_recv, k.at(dxl=1))
    zq.step(2, 0)

    xt.wait_recv()
    low = lax.broadcasted_iota(jnp.int32, (64, 128), 1) < 64
    for j in range(2):
        for zz in range(8):
            a = l_rows[j, :, pl.ds(zz // 2 * 128, 128)].astype(F32)
            b = l_rows[j, :, pl.ds((4 + zz // 2) * 128, 128)].astype(F32)
            if zz % 2:
                a = pltpu.roll(a, 64, 1)
            else:
                b = pltpu.roll(b, 64, 1)
            l_perm[zz, j] = jnp.where(low, a, b).astype(BF16)
    l_copies = []
    for o in range(1, 8):
        zz = lax.rem(z + o, 8)
        l_copies.append(send(l_perm.at[zz], l_all.at[:, z], k.at(dz=o)))
    l_all[:, z] = l_perm[z]

    zq.step(2, 1)
    zq.step(3, 0)
    y_sum(0)
    zq.step(3, 1)
    zq.step(4, 0)
    x_sum(0)
    zq.step(4, 1)
    zg[0].step(1, 0)
    zg[0].step(1, 1)
    zg[0].step(2, 0)
    zg[0].step(2, 1)
    y_sum(1)
    zg[0].step(3, 0)
    zg[0].step(3, 1)
    x_sum(1)
    zg[0].step(4, 0)
    zg[0].step(4, 1)
    for copy in l_copies:
        copy.wait_recv()
    l_t[...] = l_all[...].reshape(1024, 128).astype(F32).T.astype(BF16)
    for s in range(1, 5):
        zg[1].step(s, 0)
        zg[1].step(s, 1)

    def dot(a, b):
        return jnp.dot(a, b, preferred_element_type=F32)

    left = l_rows[...].reshape(128, 1024)
    for t in range(4):
        cols = pl.ds(t * 256, 256)
        y_rot[:, cols] = dot(left, g_full[:, :, :, cols].reshape(1024, 256)).astype(BF16)
    xm.wait_recv()
    for t in range(4):
        cols = pl.ds(t * 256, 256)
        r = dot(y_rot[...], q_full[:, :, :, cols].reshape(1024, 256)).reshape(2, 64, 256)
        r_buf[:, :, cols] = r
        for j in range(2):
            first = mom[0, xl, :, cols] if j == 0 else mom_recv[0, :, cols]
            second = mom[1, xl, :, cols] if j == 0 else mom_recv[1, :, cols]
            rj = r_buf[lax.rem(xl + j, 2), :, cols]
            first = 0.9 * first + 0.1 * rj
            second = 0.95 * second + 0.05 * rj * rj
            n_buf[lax.rem(xl + j, 2), :, cols] = (first / (jnp.sqrt(second) + 1e-8)).astype(BF16)
    normal = n_buf[...].reshape(128, 1024)
    for h in range(H):
        per = 16 // H
        for t in range(W // 256):
            slabs = q_full[...].reshape(1024, 1024)[h * W + t * 256 : h * W + (t + 1) * 256]
            part = lax.dot_general(normal, slabs, CONTRACT_LAST, preferred_element_type=F32)
            part = part.astype(BF16).reshape(2, 64, 256)
            for j in range(2):
                m_full[h, j, z, :, pl.ds(t * 256, 256)] = part[j]
        zm[h].start(1, 0)
        zm[h].start(1, 1)

    xr = send(r_buf.at[1 - xl], r_recv, k.at(dxl=1))

    def left_gram():
        rows = g_full[:, z].reshape(128, 1024)
        for t in range(4):
            slabs = g_full[...].reshape(1024, 1024)[t * 256 : (t + 1) * 256]
            part = lax.dot_general(rows, slabs, CONTRACT_LAST, preferred_element_type=F32)
            pl_buf[:, :, pl.ds(t * 256, 256)] = part.reshape(2, 64, 256)

    def right_gram():
        half = lax.div(z, 2)
        odd = lax.rem(z, 2) == 1
        wide = lax.broadcasted_iota(jnp.int32, (128, 128), 1) < 64

        for j in range(2):
            for n in range(4):
                at = pl.ds(n * 2, 2)
                a = g_full[j, at, :, pl.ds(pl.multiple_of(half * 128, 128), 128)]
                b = g_full[j, at, :, pl.ds(pl.multiple_of((half + 4) * 128, 128), 128)]
                a, b = a.reshape(128, 128).astype(F32), b.reshape(128, 128).astype(F32)
                a = jnp.where(odd, pltpu.roll(a, 64, 1), a)
                b = jnp.where(odd, b, pltpu.roll(b, 64, 1))
                g_cols[:, pl.ds((j * 4 + n) * 128, 128)] = jnp.where(wide, a, b).T.astype(BF16)
        cols = g_cols[...]
        for t in range(4):
            at = pl.ds(t * 256, 256)
            pr_buf[:, :, at] = dot(cols, g_full[:, :, :, at].reshape(1024, 256)).reshape(2, 64, 256)

    up_copies = {}
    left_t = l_t

    def update(h):
        for t in range(W // 256):
            cols = pl.ds(t * 256, 256)
            part = dot(left_t[...], m_full[h, :, :, :, cols].reshape(1024, 256))
            up_send[h, :, :, cols] = part.astype(BF16).reshape(2, 64, 256)
        up_copies[h] = send(up_send.at[h, 1 - xl], up_recv.at[h], k.at(dxl=1))

    gathers = []

    class Gather:
        def __init__(self, h):
            self.h, self.got = h, {}

        def place(self, dy, dxh, dc, half=None):
            yy, hh, cc = lax.rem(y + dy, 4), lax.rem(xh + dxh, 2), lax.rem(c + dc, 2)
            ref = out.at[(yy * 2 + hh) * 2 + cc, self.h]
            if half is not None:
                ref = ref.at[pl.ds(half * (PIECE // 2), PIECE // 2)]
            return ref

        def push(self, name, src, peer, half=None):
            dst = src
            if src is None:
                src, dst = up_piece.at[self.h], self.place(0, 0, 0)
            self.got[name] = send(src, dst, peer)

        def begin(self):
            self.keep = local(up_piece.at[self.h], self.place(0, 0, 0))
            self.push("x", None, k.at(dxh=1))
            self.push((0, 1), None, k.at(dy=1))
            self.push((0, 3), None, k.at(dy=3))
            self.push((0, 0, "c"), None, k.at(dc=1))

        def x_arrive(self):
            self.got["x"].wait_recv()
            at = self.place(0, 1, 0)
            self.push((1, 1), at, k.at(dy=1))
            self.push((1, 3), at, k.at(dy=3))
            self.push((1, 0, "c"), at, k.at(dc=1))

        def relay(self, e):
            self.got[e, 1].wait_recv()
            self.push((e, 2, 0), self.place(3, e, 0, 0), k.at(dy=1))
            self.push((e, 1, "c"), self.place(3, e, 0), k.at(dc=1))
            self.got[e, 3].wait_recv()
            self.push((e, 2, 1), self.place(1, e, 0, 1), k.at(dy=3))
            self.push((e, 3, "c"), self.place(1, e, 0), k.at(dc=1))

        def finish(self, e):
            self.got[e, 2, 0].wait_recv()
            self.got[e, 2, 1].wait_recv()
            self.push((e, 2, "c"), self.place(2, e, 0), k.at(dc=1))

        def end(self):
            for e in range(2):
                for o in range(4):
                    self.got[e, o, "c"].wait_recv()
            self.keep.wait()

    gathers = [Gather(h) for h in range(H)]

    def pack_up(h):
        up_copies[h].wait_recv()
        n = W // 128
        for b in range(2):
            for t in range(n):
                cols = pl.ds(t * 128, 128)
                mine, theirs = up_send[h, xl, :, cols], up_recv[h, :, cols]
                piece = jnp.where(xl == b, mine.astype(F32), theirs.astype(F32))
                pack[pl.ds(t * 2 + b, 64, stride=2 * n), :] = piece
        up_piece[h] = pack[...].astype(BF16)
        gathers[h].begin()

    left_gram()
    xl_copy = send(pl_buf.at[1 - xl], pl_recv, k.at(dxl=1))
    zm[0].step(1, 0)
    zm[0].step(1, 1)
    zm[1].step(1, 0)
    zm[1].step(1, 1)
    right_gram()
    xr_copy = send(pr_buf.at[1 - xl], pr_recv, k.at(dxl=1))
    for s in (2, 3):
        for h in range(H):
            zm[h].step(s, 0)
            zm[h].step(s, 1)
    zm[0].step(4, 0)
    zm[0].step(4, 1)
    update(0)
    zm[1].step(4, 0)
    zm[1].step(4, 1)
    pack_up(0)
    update(1)
    gathers[0].x_arrive()
    pack_up(1)
    gathers[0].relay(0)

    def weave(dst, buf, received):
        for b in range(2):
            for t in range(8):
                cols = pl.ds(t * 128, 128)
                dst[pl.ds(t * 2 + b, 64, stride=16), :] = jnp.where(
                    xl == b, buf[xl, :, cols], received[:, cols]
                )

    xr.wait_recv()
    weave(rot, r_buf, r_recv)
    gathers[1].x_arrive()
    gathers[0].relay(1)
    gathers[0].finish(0)
    xl_copy.wait_recv()
    weave(pleft, pl_buf, pl_recv)
    gathers[1].relay(0)
    gathers[0].finish(1)
    xr_copy.wait_recv()
    weave(pright, pr_buf, pr_recv)
    gathers[1].relay(1)
    gathers[1].finish(0)
    gathers[1].finish(1)
    gathers[0].end()
    gathers[1].end()
    for copy in unsent:
        copy.wait_send()


def per_device(grads, left_basis_t, right_basis, first, second, left_gram, right_gram):
    g = rows_view(grads[0]).reshape(64, 8, 2, 16, 128)
    lt, qr = (rows_view(a).reshape(64, 16, 128) for a in (left_basis_t, right_basis))
    m1, m2, lg, rg = (rows_view(a).reshape(1024, 128) for a in (first, second, left_gram, right_gram))
    any_spec, vmem = pl.BlockSpec(memory_space=pl.ANY), pl.BlockSpec(memory_space=pltpu.VMEM)
    shape = jax.ShapeDtypeStruct
    v = pltpu.VMEM
    out, rot, pleft, pright = pl.pallas_call(
        kernel,
        out_shape=[shape((16, H, PIECE, 128), BF16)] + [shape((1024, 128), F32)] * 3,
        in_specs=[any_spec] * 5,
        out_specs=[any_spec] + [vmem] * 3,
        scratch_shapes=[
            v((2, 64, 16, 128), BF16),
            v((2, 1024, 128), F32),
            v((2, 32, 8, 16, 128), BF16),
            v((2, 32, 8, 16, 128), BF16),
            v((2, 4, 32, 2, 16, 128), BF16),
            v((2, 3, 32, 2, 16, 128), BF16),
            v((2, 2, 2, 32, 1024), BF16),
            v((2, 3, 32, 1024), BF16),
            v((1024, 128), F32),
            v((2, 64, 1024), BF16),
            v((2, 8, 64, 1024), BF16),
            v((2, 64, 1024), BF16),
            v((2, 64, 1024), BF16),
            v((8, 2, 64, 128), BF16),
            v((2, 8, 64, 128), BF16),
            v((128, 1024), BF16),
            v((2, 8, 64, 1024), BF16),
            v((2, 2, 64, 1024), F32),
            v((2, 64, 1024), F32),
            v((128, 1024), BF16),
            v((2, 64, 1024), BF16),
            v((H, 2, 8, 64, W), BF16),
            v((2, 64, 1024), F32),
            v((64, 1024), F32),
            v((2, 64, 1024), F32),
            v((64, 1024), F32),
            v((2, 64, 1024), F32),
            v((64, 1024), F32),
            v((128, 1024), BF16),
            v((H, 2, 64, W), BF16),
            v((H, 64, W), BF16),
            v((PIECE, 128), F32),
            v((H, PIECE, 128), BF16),
            pltpu.SemaphoreType.DMA((NCOPY,)),
            pltpu.SemaphoreType.DMA((NCOPY,)),
            pltpu.SemaphoreType.DMA((16,)),
        ],
        compiler_params=pltpu.CompilerParams(
            collective_id=0, has_side_effects=True, vmem_limit_bytes=40 << 20
        ),
        name="soap",
    )(g, lt, qr, m1, m2)
    n1 = 0.9 * m1 + 0.1 * rot
    n2 = 0.95 * m2 + 0.05 * rot * rot
    nl = 0.95 * lg + 0.05 * pleft
    nr = 0.95 * rg + 0.05 * pright
    update = out.reshape(16, H, 64, PIECE // 64, 128).transpose(2, 0, 1, 3, 4)
    update = update.reshape(64, 128, 2, 128).transpose(0, 2, 1, 3).reshape(64, 2, 16384)

    def back(a):
        return a.reshape(64, 8, 2, 128).transpose(0, 2, 1, 3).reshape(64, 2, 1024)

    return update, back(n1), back(n2), back(nl), back(nr)


def solution(mesh):
    sharded = P("fsdp", None, "dp")
    return jax.shard_map(
        per_device,
        mesh=mesh,
        in_specs=(P("dp", "fsdp", None, None),) + (sharded,) * 6,
        out_specs=(P("fsdp", None, None),) + (sharded,) * 4,
        check_vma=False,
    )
```

```python
import jax
import jax.numpy as jnp
from jax import lax
from jax.experimental import pallas as pl
from jax.experimental.pallas import tpu as pltpu
from jax.sharding import PartitionSpec as P

MESH = pl.DeviceIdType.MESH
F32, BF16 = jnp.float32, jnp.bfloat16
NCOPY = 200
H = 2
W = 1024 // H
PIECE = 1024 // H
CONTRACT_LAST = (((1,), (1,)), ((), ()))


def rows_view(x):
    i, b, n = x.shape
    return x.reshape(i, b, n // 128, 128).transpose(0, 2, 1, 3)


class Peers:
    def __init__(self):
        dp, fs = lax.axis_index("dp"), lax.axis_index("fsdp")
        self.y, self.xh, self.c = lax.div(dp, 4), lax.rem(lax.div(dp, 2), 2), lax.rem(dp, 2)
        self.xl, self.z = lax.div(fs, 8), lax.rem(fs, 8)

    def at(self, dy=0, dxh=0, dc=0, dxl=0, dz=0):
        y, xh, c = lax.rem(self.y + dy, 4), lax.rem(self.xh + dxh, 2), lax.rem(self.c + dc, 2)
        xl, z = lax.rem(self.xl + dxl, 2), lax.rem(self.z + dz, 8)
        return ((y * 2 + xh) * 2 + c, xl * 8 + z)


def kernel(
    g, lt, qr, m1, m2, lg, rg,
    out, new_first_out, new_second_out, new_left_out, new_right_out,
    new_first, new_second, new_left, new_right, gram_in, in_bf, mom_in, own, other, summed, y_recv, x_send, x_recv, acc,
    q_split, q_full, l_split, l_rows, l_perm, l_all, l_t,
    g_full, mom, mom_recv, y_rot, n_buf, m_full, r_buf, r_recv, pl_buf, pl_recv, pr_buf, pr_recv,
    g_cols, up_send, up_recv, pack, up_piece,
    ss, rs, ls,
):
    k = Peers()
    y, xh, c, xl, z = k.y, k.xh, k.c, k.xl, k.z
    count = [0, 0]
    unsent = []

    def remote(src, dst, peer):
        n = count[0]
        count[0] += 1
        copy = pltpu.make_async_remote_copy(
            src, dst, ss.at[n], rs.at[n], device_id=peer, device_id_type=MESH
        )
        unsent.append(copy)
        return copy

    def send(src, dst, peer):
        copy = remote(src, dst, peer)
        copy.start()
        return copy

    def local(src, dst):
        n = count[1]
        count[1] += 1
        copy = pltpu.make_async_copy(src, dst, ls.at[n])
        copy.start()
        return copy

    partners = (
        [k.at(dc=1), k.at(dxl=1), k.at(dxh=1), k.at(dxh=1, dxl=1)]
        + [k.at(dy=o) for o in (1, 2, 3)]
        + [k.at(dz=o) for o in range(1, 8)]
    )
    barrier = pltpu.get_barrier_semaphore()
    for peer in partners:
        pl.semaphore_signal(barrier, inc=1, device_id=peer, device_id_type=MESH)

    load_q = local(qr, in_bf.at[0])
    load_l = local(lt, in_bf.at[1])
    load_own = [local(g.at[pl.ds(q * 32, 32), :, c], own.at[q]) for q in range(2)]
    load_m = [local(m1, mom_in.at[0]), local(m2, mom_in.at[1])]
    load_g = [local(lg, gram_in.at[0]), local(rg, gram_in.at[1])]

    def split_bf(src, dst):
        acc[...] = src[...].reshape(1024, 128).astype(F32)
        for b in range(2):
            for t in range(8):
                dst[b, :, pl.ds(t * 128, 128)] = acc[pl.ds(t * 2 + b, 64, stride=16), :].astype(BF16)

    class ZGather:
        def __init__(self, ref):
            self.ref, self.copies = ref, {}

        def start(self, s, j):
            for d in (1, -1):
                if s == 4 and j != (d == -1):
                    continue
                at = self.ref(lax.rem(xl + j, 2), lax.rem(z - d * (s - 1) + 8, 8))
                self.copies[s, j, d] = send(at, at, k.at(dz=d % 8))

        def arrive(self, s, j):
            for d in (1, -1):
                if (s, j, d) in self.copies:
                    self.copies[s, j, d].wait_recv()

        def step(self, s, j):
            self.arrive(s, j)
            if s < 4:
                self.start(s + 1, j)

    zq = ZGather(lambda j, zz: q_full.at[j, zz])
    zg = [
        ZGather(lambda j, zz, q=q: g_full.at[j, zz, pl.ds(q * 32, 32), :]) for q in range(2)
    ]
    zm = [ZGather(lambda j, zz, h=h: m_full.at[h, j, zz]) for h in range(H)]

    load_q.wait()
    split_bf(in_bf.at[0], q_split)
    q_full[xl, z] = q_split[xl]
    pl.semaphore_wait(barrier, len(partners))

    core = [send(g.at[pl.ds(q * 32, 32), :, 1 - c], other.at[q], k.at(dc=1)) for q in range(2)]
    xq = send(q_split.at[1 - xl], q_full.at[xl, z], k.at(dxl=1))
    zq.start(1, 0)
    load_l.wait()
    split_bf(in_bf.at[1], l_split)
    xt = send(l_split.at[1 - xl], l_rows.at[xl], k.at(dxl=1))
    l_rows[xl] = l_split[xl]

    y_copies = {}

    def core_sum(q):
        load_own[q].wait()
        core[q].wait_recv()
        for o in (2, 1, 3, 0):
            yy = lax.rem(y + o, 4)

            @pl.loop(0, 8)
            def _(i):
                at = (q, pl.ds(i * 4, 4), pl.ds(yy * 2, 2))
                total = own[at].astype(F32) + other[at].astype(F32)
                summed[q, yy, pl.ds(i * 4, 4)] = total.astype(BF16)

            if o:
                y_copies[q, o] = send(summed.at[q, yy], y_recv.at[q, o - 1], k.at(dy=o))

    x_copies = {}

    def y_sum(q):
        for o in (1, 2, 3):
            y_copies[q, o].wait_recv()

        @pl.loop(0, 8)
        def _(i):
            at = pl.ds(i * 4, 4)
            total = summed[q, y, at].astype(F32)
            for o in range(3):
                total += y_recv[q, o, at].astype(F32)
            acc[pl.ds(i * 128, 128), :] = total.reshape(128, 128)

        for e in range(2):
            for b in range(2):
                for t in range(8):
                    x_send[q, e, b, :, pl.ds(t * 128, 128)] = acc[
                        pl.ds(e * 16 + t * 2 + b, 32, stride=32), :
                    ].astype(BF16)
        for n, (dh, dl) in enumerate(((1, 1), (1, 0), (0, 1))):
            x_copies[q, n] = send(
                x_send.at[q, lax.rem(xh + dh, 2), lax.rem(xl + dl, 2)],
                x_recv.at[q, n],
                k.at(dxh=dh, dxl=dl),
            )

    def x_sum(q):
        at = pl.ds(q * 32, 32)
        x_copies[q, 1].wait_recv()
        g_full[xl, z, at] = (
            x_send[q, xh, xl].astype(F32) + x_recv[q, 1].astype(F32)
        ).astype(BF16)
        zg[q].start(1, 0)
        x_copies[q, 0].wait_recv()
        x_copies[q, 2].wait_recv()
        g_full[1 - xl, z, at] = (x_recv[q, 0].astype(F32) + x_recv[q, 2].astype(F32)).astype(BF16)
        zg[q].start(1, 1)

    core_sum(0)
    xq.wait_recv()
    zq.start(1, 1)
    zq.step(1, 0)
    core_sum(1)
    zq.step(1, 1)

    for n in range(2):
        load_m[n].wait()
        for b in range(2):
            for t in range(8):
                mom[n, b, :, pl.ds(t * 128, 128)] = mom_in[n, pl.ds(t * 2 + b, 64, stride=16), :]
    xm = send(mom.at[:, 1 - xl], mom_recv, k.at(dxl=1))
    zq.step(2, 0)

    xt.wait_recv()
    low = lax.broadcasted_iota(jnp.int32, (64, 128), 1) < 64
    for j in range(2):
        for zz in range(8):
            a = l_rows[j, :, pl.ds(zz // 2 * 128, 128)].astype(F32)
            b = l_rows[j, :, pl.ds((4 + zz // 2) * 128, 128)].astype(F32)
            if zz % 2:
                a = pltpu.roll(a, 64, 1)
            else:
                b = pltpu.roll(b, 64, 1)
            l_perm[zz, j] = jnp.where(low, a, b).astype(BF16)
    l_copies = []
    for o in range(1, 8):
        zz = lax.rem(z + o, 8)
        l_copies.append(send(l_perm.at[zz], l_all.at[:, z], k.at(dz=o)))
    l_all[:, z] = l_perm[z]

    zq.step(2, 1)
    zq.step(3, 0)
    y_sum(0)
    zq.step(3, 1)
    zq.step(4, 0)
    x_sum(0)
    zq.step(4, 1)
    zg[0].step(1, 0)
    zg[0].step(1, 1)
    zg[0].step(2, 0)
    zg[0].step(2, 1)
    y_sum(1)
    zg[0].step(3, 0)
    zg[0].step(3, 1)
    x_sum(1)
    zg[0].step(4, 0)
    zg[0].step(4, 1)
    for copy in l_copies:
        copy.wait_recv()
    l_t[...] = l_all[...].reshape(1024, 128).astype(F32).T.astype(BF16)
    for s in range(1, 5):
        zg[1].step(s, 0)
        zg[1].step(s, 1)

    def dot(a, b):
        return jnp.dot(a, b, preferred_element_type=F32)

    left = l_rows[...].reshape(128, 1024)
    for t in range(4):
        cols = pl.ds(t * 256, 256)
        y_rot[:, cols] = dot(left, g_full[:, :, :, cols].reshape(1024, 256)).astype(BF16)
    xm.wait_recv()
    for t in range(4):
        cols = pl.ds(t * 256, 256)
        r = dot(y_rot[...], q_full[:, :, :, cols].reshape(1024, 256)).reshape(2, 64, 256)
        r_buf[:, :, cols] = r
        for j in range(2):
            first = mom[0, xl, :, cols] if j == 0 else mom_recv[0, :, cols]
            second = mom[1, xl, :, cols] if j == 0 else mom_recv[1, :, cols]
            rj = r_buf[lax.rem(xl + j, 2), :, cols]
            first = 0.9 * first + 0.1 * rj
            second = 0.95 * second + 0.05 * rj * rj
            n_buf[lax.rem(xl + j, 2), :, cols] = (first / (jnp.sqrt(second) + 1e-8)).astype(BF16)
    normal = n_buf[...].reshape(128, 1024)
    for h in range(H):
        per = 16 // H
        for t in range(W // 256):
            slabs = q_full[...].reshape(1024, 1024)[h * W + t * 256 : h * W + (t + 1) * 256]
            part = lax.dot_general(normal, slabs, CONTRACT_LAST, preferred_element_type=F32)
            part = part.astype(BF16).reshape(2, 64, 256)
            for j in range(2):
                m_full[h, j, z, :, pl.ds(t * 256, 256)] = part[j]
        zm[h].start(1, 0)
        zm[h].start(1, 1)

    xr = send(r_buf.at[1 - xl], r_recv, k.at(dxl=1))

    def left_gram():
        rows = g_full[:, z].reshape(128, 1024)
        for t in range(4):
            slabs = g_full[...].reshape(1024, 1024)[t * 256 : (t + 1) * 256]
            part = lax.dot_general(rows, slabs, CONTRACT_LAST, preferred_element_type=F32)
            pl_buf[:, :, pl.ds(t * 256, 256)] = part.reshape(2, 64, 256)

    def right_gram():
        half = lax.div(z, 2)
        odd = lax.rem(z, 2) == 1
        wide = lax.broadcasted_iota(jnp.int32, (128, 128), 1) < 64

        for j in range(2):
            for n in range(4):
                at = pl.ds(n * 2, 2)
                a = g_full[j, at, :, pl.ds(pl.multiple_of(half * 128, 128), 128)]
                b = g_full[j, at, :, pl.ds(pl.multiple_of((half + 4) * 128, 128), 128)]
                a, b = a.reshape(128, 128).astype(F32), b.reshape(128, 128).astype(F32)
                a = jnp.where(odd, pltpu.roll(a, 64, 1), a)
                b = jnp.where(odd, b, pltpu.roll(b, 64, 1))
                g_cols[:, pl.ds((j * 4 + n) * 128, 128)] = jnp.where(wide, a, b).T.astype(BF16)
        cols = g_cols[...]
        for t in range(4):
            at = pl.ds(t * 256, 256)
            pr_buf[:, :, at] = dot(cols, g_full[:, :, :, at].reshape(1024, 256)).reshape(2, 64, 256)

    up_copies = {}
    left_t = l_t

    def update(h):
        for t in range(W // 256):
            cols = pl.ds(t * 256, 256)
            part = dot(left_t[...], m_full[h, :, :, :, cols].reshape(1024, 256))
            up_send[h, :, :, cols] = part.astype(BF16).reshape(2, 64, 256)
        up_copies[h] = send(up_send.at[h, 1 - xl], up_recv.at[h], k.at(dxl=1))

    gathers = []

    class Gather:
        def __init__(self, h):
            self.h, self.got = h, {}

        def place(self, dy, dxh, dc, half=None):
            yy, hh, cc = lax.rem(y + dy, 4), lax.rem(xh + dxh, 2), lax.rem(c + dc, 2)
            ref = out.at[(yy * 2 + hh) * 2 + cc, self.h]
            if half is not None:
                ref = ref.at[pl.ds(half * (PIECE // 2), PIECE // 2)]
            return ref

        def push(self, name, src, peer, half=None):
            dst = src
            if src is None:
                src, dst = up_piece.at[self.h], self.place(0, 0, 0)
            self.got[name] = send(src, dst, peer)

        def begin(self):
            self.keep = local(up_piece.at[self.h], self.place(0, 0, 0))
            self.push("x", None, k.at(dxh=1))
            self.push((0, 1), None, k.at(dy=1))
            self.push((0, 3), None, k.at(dy=3))
            self.push((0, 0, "c"), None, k.at(dc=1))

        def x_arrive(self):
            self.got["x"].wait_recv()
            at = self.place(0, 1, 0)
            self.push((1, 1), at, k.at(dy=1))
            self.push((1, 3), at, k.at(dy=3))
            self.push((1, 0, "c"), at, k.at(dc=1))

        def relay(self, e):
            self.got[e, 1].wait_recv()
            self.push((e, 2, 0), self.place(3, e, 0, 0), k.at(dy=1))
            self.push((e, 1, "c"), self.place(3, e, 0), k.at(dc=1))
            self.got[e, 3].wait_recv()
            self.push((e, 2, 1), self.place(1, e, 0, 1), k.at(dy=3))
            self.push((e, 3, "c"), self.place(1, e, 0), k.at(dc=1))

        def finish(self, e):
            self.got[e, 2, 0].wait_recv()
            self.got[e, 2, 1].wait_recv()
            self.push((e, 2, "c"), self.place(2, e, 0), k.at(dc=1))

        def end(self):
            for e in range(2):
                for o in range(4):
                    self.got[e, o, "c"].wait_recv()
            self.keep.wait()

    gathers = [Gather(h) for h in range(H)]

    def pack_up(h):
        up_copies[h].wait_recv()
        n = W // 128
        for b in range(2):
            for t in range(n):
                cols = pl.ds(t * 128, 128)
                mine, theirs = up_send[h, xl, :, cols], up_recv[h, :, cols]
                piece = jnp.where(xl == b, mine.astype(F32), theirs.astype(F32))
                pack[pl.ds(t * 2 + b, 64, stride=2 * n), :] = piece
        up_piece[h] = pack[...].astype(BF16)
        gathers[h].begin()

    left_gram()
    xl_copy = send(pl_buf.at[1 - xl], pl_recv, k.at(dxl=1))
    zm[0].step(1, 0)
    zm[0].step(1, 1)
    zm[1].step(1, 0)
    zm[1].step(1, 1)
    right_gram()
    xr_copy = send(pr_buf.at[1 - xl], pr_recv, k.at(dxl=1))
    for s in (2, 3):
        for h in range(H):
            zm[h].step(s, 0)
            zm[h].step(s, 1)
    zm[0].step(4, 0)
    zm[0].step(4, 1)
    update(0)
    zm[1].step(4, 0)
    zm[1].step(4, 1)
    pack_up(0)
    update(1)
    gathers[0].x_arrive()
    pack_up(1)
    gathers[0].relay(0)

    def woven(buf, received, b, t):
        cols = pl.ds(t * 128, 128)
        return jnp.where(xl == b, buf[xl, :, cols], received[:, cols])

    def new_moments():
        for b in range(2):
            for t in range(8):
                at = pl.ds(t * 2 + b, 64, stride=16)
                r = woven(r_buf, r_recv, b, t)
                new_first[at, :] = 0.9 * mom_in[0, at, :] + 0.1 * r
                new_second[at, :] = 0.95 * mom_in[1, at, :] + 0.05 * r * r

    def new_gram(dst, n, buf, received):
        load_g[n].wait()
        for b in range(2):
            for t in range(8):
                at = pl.ds(t * 2 + b, 64, stride=16)
                dst[at, :] = 0.95 * gram_in[n, at, :] + 0.05 * woven(buf, received, b, t)

    xr.wait_recv()
    new_moments()
    results = [local(new_first, new_first_out), local(new_second, new_second_out)]
    gathers[1].x_arrive()
    gathers[0].relay(1)
    gathers[0].finish(0)
    xl_copy.wait_recv()
    new_gram(new_left, 0, pl_buf, pl_recv)
    results.append(local(new_left, new_left_out))
    gathers[1].relay(0)
    gathers[0].finish(1)
    xr_copy.wait_recv()
    new_gram(new_right, 1, pr_buf, pr_recv)
    results.append(local(new_right, new_right_out))
    gathers[1].relay(1)
    gathers[1].finish(0)
    gathers[1].finish(1)
    gathers[0].end()
    gathers[1].end()
    for copy in results:
        copy.wait()
    for copy in unsent:
        copy.wait_send()


def write_out(part, n1, n2, nl, nr, update, o1, o2, ol, orr, held, whole, rest, sems):
    loads, copies = [], []
    for n in range(4):
        at = pl.ds(n * 4, 4)
        loads.append(pltpu.make_async_copy(part.at[at], held.at[at], sems.at[n]))
        loads[-1].start()
    for n, src in enumerate((n1, n2, nl, nr)):
        loads.append(pltpu.make_async_copy(src, rest.at[n], sems.at[4 + n]))
        loads[-1].start()
    for n in range(4):
        loads[n].wait()

        @pl.loop(n * 4, n * 4 + 4)
        def _(d):
            for r in range(4):
                rows = [
                    held[d, h, pl.ds(r * 128, 128), :].astype(F32).reshape(16, 8, 128)
                    for h in range(H)
                ]
                whole[pl.ds(r * 16, 16), d] = jnp.concatenate(rows, axis=1).astype(BF16)

        at = (slice(None), pl.ds(n * 4, 4))
        copies.append(pltpu.make_async_copy(whole.at[at], update.at[at], sems.at[8 + n]))
        copies[-1].start()
    for n, dst in enumerate((o1, o2, ol, orr)):
        loads[4 + n].wait()
        copies.append(pltpu.make_async_copy(rest.at[n], dst, sems.at[n]))
        copies[-1].start()
    for copy in copies:
        copy.wait()


def per_device(grads, left_basis_t, right_basis, first, second, left_gram, right_gram):
    g = rows_view(grads[0]).reshape(64, 8, 2, 16, 128)
    lt, qr = (rows_view(a).reshape(64, 16, 128) for a in (left_basis_t, right_basis))
    m1, m2, lg, rg = (rows_view(a).reshape(1024, 128) for a in (first, second, left_gram, right_gram))
    hbm = pl.BlockSpec(memory_space=pl.ANY)
    shape = jax.ShapeDtypeStruct
    v = pltpu.VMEM
    done = pl.pallas_call(
        kernel,
        out_shape=[shape((16, H, PIECE, 128), BF16)] + [shape((1024, 128), F32)] * 4,
        in_specs=[hbm] * 7,
        out_specs=[hbm] * 5,
        scratch_shapes=[
            v((1024, 128), F32),
            v((1024, 128), F32),
            v((1024, 128), F32),
            v((1024, 128), F32),
            v((2, 1024, 128), F32),
            v((2, 64, 16, 128), BF16),
            v((2, 1024, 128), F32),
            v((2, 32, 8, 16, 128), BF16),
            v((2, 32, 8, 16, 128), BF16),
            v((2, 4, 32, 2, 16, 128), BF16),
            v((2, 3, 32, 2, 16, 128), BF16),
            v((2, 2, 2, 32, 1024), BF16),
            v((2, 3, 32, 1024), BF16),
            v((1024, 128), F32),
            v((2, 64, 1024), BF16),
            v((2, 8, 64, 1024), BF16),
            v((2, 64, 1024), BF16),
            v((2, 64, 1024), BF16),
            v((8, 2, 64, 128), BF16),
            v((2, 8, 64, 128), BF16),
            v((128, 1024), BF16),
            v((2, 8, 64, 1024), BF16),
            v((2, 2, 64, 1024), F32),
            v((2, 64, 1024), F32),
            v((128, 1024), BF16),
            v((2, 64, 1024), BF16),
            v((H, 2, 8, 64, W), BF16),
            v((2, 64, 1024), F32),
            v((64, 1024), F32),
            v((2, 64, 1024), F32),
            v((64, 1024), F32),
            v((2, 64, 1024), F32),
            v((64, 1024), F32),
            v((128, 1024), BF16),
            v((H, 2, 64, W), BF16),
            v((H, 64, W), BF16),
            v((PIECE, 128), F32),
            v((H, PIECE, 128), BF16),
            pltpu.SemaphoreType.DMA((NCOPY,)),
            pltpu.SemaphoreType.DMA((NCOPY,)),
            pltpu.SemaphoreType.DMA((16,)),
        ],
        compiler_params=pltpu.CompilerParams(
            collective_id=0, has_side_effects=True, vmem_limit_bytes=56 << 20
        ),
        name="soap",
    )(g, lt, qr, m1, m2, lg, rg)
    update, *rest = pl.pallas_call(
        write_out,
        out_shape=[shape((64, 16, 16, 128), BF16)] + [shape((1024, 128), F32)] * 4,
        in_specs=[hbm] * 5,
        out_specs=[hbm] * 5,
        scratch_shapes=[
            v((16, H, PIECE, 128), BF16),
            v((64, 16, 16, 128), BF16),
            v((4, 1024, 128), F32),
            pltpu.SemaphoreType.DMA((12,)),
        ],
        compiler_params=pltpu.CompilerParams(vmem_limit_bytes=56 << 20),
        name="write_out",
    )(*done)
    update = update.reshape(64, 128, 2, 128).transpose(0, 2, 1, 3).reshape(64, 2, 16384)

    def back(a):
        return a.reshape(64, 8, 2, 128).transpose(0, 2, 1, 3).reshape(64, 2, 1024)

    return (update, *(back(a) for a in rest))


def solution(mesh):
    sharded = P("fsdp", None, "dp")
    return jax.shard_map(
        per_device,
        mesh=mesh,
        in_specs=(P("dp", "fsdp", None, None),) + (sharded,) * 6,
        out_specs=(P("fsdp", None, None),) + (sharded,) * 4,
        check_vma=False,
    )
```

```python
import jax
import jax.numpy as jnp
from jax import lax
from jax.experimental import pallas as pl
from jax.experimental.pallas import tpu as pltpu
from jax.sharding import PartitionSpec as P

MESH = pl.DeviceIdType.MESH
F32, BF16 = jnp.float32, jnp.bfloat16
NCOPY = 256
H = 4
W = 1024 // H
PIECE = 1024 // H
CONTRACT_LAST = (((1,), (1,)), ((), ()))


def rows_view(x):
    i, b, n = x.shape
    return x.reshape(i, b, n // 128, 128).transpose(0, 2, 1, 3)


class Peers:
    def __init__(self):
        dp, fs = lax.axis_index("dp"), lax.axis_index("fsdp")
        self.y, self.xh, self.c = lax.div(dp, 4), lax.rem(lax.div(dp, 2), 2), lax.rem(dp, 2)
        self.xl, self.z = lax.div(fs, 8), lax.rem(fs, 8)

    def at(self, dy=0, dxh=0, dc=0, dxl=0, dz=0):
        y, xh, c = lax.rem(self.y + dy, 4), lax.rem(self.xh + dxh, 2), lax.rem(self.c + dc, 2)
        xl, z = lax.rem(self.xl + dxl, 2), lax.rem(self.z + dz, 8)
        return ((y * 2 + xh) * 2 + c, xl * 8 + z)


def kernel(
    g, lt, qr, m1, m2, lg, rg,
    out, new_first_out, new_second_out, new_left_out, new_right_out,
    new_first, new_second, new_left, new_right, gram_in, in_bf, mom_in, own, other, summed, y_recv, y_relay, x_send, x_recv, acc,
    q_split, q_full, l_split, l_rows, l_perm, l_all, l_t,
    g_full, mom, mom_recv, y_rot, n_buf, m_full, r_buf, r_recv, pl_buf, pl_recv, pr_buf, pr_recv,
    g_cols, up_send, up_recv, pack, up_piece,
    ss, rs, ls,
):
    k = Peers()
    y, xh, c, xl, z = k.y, k.xh, k.c, k.xl, k.z
    count = [0, 0]
    unsent = []

    def remote(src, dst, peer):
        n = count[0]
        count[0] += 1
        copy = pltpu.make_async_remote_copy(
            src, dst, ss.at[n], rs.at[n], device_id=peer, device_id_type=MESH
        )
        unsent.append(copy)
        return copy

    def send(src, dst, peer):
        copy = remote(src, dst, peer)
        copy.start()
        return copy

    def local(src, dst):
        n = count[1]
        count[1] += 1
        copy = pltpu.make_async_copy(src, dst, ls.at[n])
        copy.start()
        return copy

    partners = (
        [k.at(dc=1), k.at(dxl=1), k.at(dxh=1), k.at(dxh=1, dxl=1)]
        + [k.at(dy=o) for o in (1, 2, 3)]
        + [k.at(dz=o) for o in range(1, 8)]
    )
    barrier = pltpu.get_barrier_semaphore()
    for peer in partners:
        pl.semaphore_signal(barrier, inc=1, device_id=peer, device_id_type=MESH)

    load_q = local(qr, in_bf.at[0])
    load_l = local(lt, in_bf.at[1])
    load_own = [local(g.at[pl.ds(q * 32, 32), :, c], own.at[q]) for q in range(2)]
    load_m = [local(m1, mom_in.at[0]), local(m2, mom_in.at[1])]
    load_g = [local(lg, gram_in.at[0]), local(rg, gram_in.at[1])]

    def split_bf(src, dst):
        acc[...] = src[...].reshape(1024, 128).astype(F32)
        for b in range(2):
            for t in range(8):
                dst[b, :, pl.ds(t * 128, 128)] = acc[pl.ds(t * 2 + b, 64, stride=16), :].astype(BF16)

    class ZGather:
        def __init__(self, ref):
            self.ref, self.copies = ref, {}

        def start(self, s, j):
            for d in (1, -1):
                if s == 4 and j != (d == -1):
                    continue
                at = self.ref(lax.rem(xl + j, 2), lax.rem(z - d * (s - 1) + 8, 8))
                self.copies[s, j, d] = send(at, at, k.at(dz=d % 8))

        def arrive(self, s, j):
            for d in (1, -1):
                if (s, j, d) in self.copies:
                    self.copies[s, j, d].wait_recv()

        def step(self, s, j):
            self.arrive(s, j)
            if s < 4:
                self.start(s + 1, j)

        def steps(self, s):
            self.step(s, 0)
            self.step(s, 1)

    zq = ZGather(lambda j, zz: q_full.at[j, zz])
    zg = [
        ZGather(lambda j, zz, q=q: g_full.at[j, zz, pl.ds(q * 32, 32), :]) for q in range(2)
    ]
    zm = [ZGather(lambda j, zz, h=h: m_full.at[h, j, zz]) for h in range(H)]

    pl.semaphore_wait(barrier, len(partners))
    core = [send(g.at[pl.ds(q * 32, 32), :, 1 - c], other.at[q], k.at(dc=1)) for q in range(2)]
    load_q.wait()
    split_bf(in_bf.at[0], q_split)
    q_full[xl, z] = q_split[xl]
    xq = send(q_split.at[1 - xl], q_full.at[xl, z], k.at(dxl=1))
    zq.start(1, 0)
    y_copies = {}

    def core_sum(q):
        load_own[q].wait()
        core[q].wait_recv()
        for o in (2, 1, 3, 0):
            yy = lax.rem(y + o, 4)

            @pl.loop(0, 8)
            def _(i):
                at = (q, pl.ds(i * 4, 4), pl.ds(yy * 2, 2))
                total = (own[at].astype(F32) + other[at].astype(F32)).astype(BF16)
                for e in range(2):
                    summed[q, yy, e, pl.ds(i * 4, 4)] = total[:, e]

            if o == 2:
                y_copies[q, "far", 1] = send(summed.at[q, yy, 0], y_relay.at[q, 0], k.at(dy=1))
                y_copies[q, "far", 3] = send(summed.at[q, yy, 1], y_relay.at[q, 1], k.at(dy=3))
            elif o:
                e = 1 if o == 1 else 0
                y_copies[q, "near", o] = send(
                    summed.at[q, yy, e], y_recv.at[q, o // 2, e], k.at(dy=o)
                )

    def y_pass(q):
        for e, o in ((0, 1), (1, 3)):
            y_copies[q, "far", o].wait_recv()
            yy = lax.rem(y + o, 4)

            @pl.loop(0, 4)
            def _(i):
                at = pl.ds(i * 8, 8)
                total = summed[q, yy, e, at].astype(F32) + y_relay[q, e, at].astype(F32)
                y_relay[q, e, at] = total.astype(BF16)

            y_copies[q, "sum", o] = send(y_relay.at[q, e], y_recv.at[q, o // 2, e], k.at(dy=o))

    x_copies = {}

    def y_sum(q):
        for o in (1, 3):
            y_copies[q, "near", o].wait_recv()
            y_copies[q, "sum", o].wait_recv()
        for e in range(2):

            @pl.loop(0, 4)
            def _(i):
                at = pl.ds(i * 8, 8)
                total = summed[q, y, e, at].astype(F32)
                for o in range(2):
                    total += y_recv[q, o, e, at].astype(F32)
                acc[pl.ds(e * 512 + i * 128, 128), :] = total.reshape(128, 128)

            for b in range(2):
                for t in range(8):
                    x_send[q, e, b, :, pl.ds(t * 128, 128)] = acc[
                        pl.ds(e * 512 + t * 2 + b, 32, stride=16), :
                    ].astype(BF16)
        for n, (dh, dl) in enumerate(((1, 1), (1, 0), (0, 1))):
            x_copies[q, n] = send(
                x_send.at[q, lax.rem(xh + dh, 2), lax.rem(xl + dl, 2)],
                x_recv.at[q, n],
                k.at(dxh=dh, dxl=dl),
            )

    def x_sum(q):
        at = pl.ds(q * 32, 32)
        x_copies[q, 1].wait_recv()
        g_full[xl, z, at] = (
            x_send[q, xh, xl].astype(F32) + x_recv[q, 1].astype(F32)
        ).astype(BF16)
        zg[q].start(1, 0)
        x_copies[q, 0].wait_recv()
        x_copies[q, 2].wait_recv()
        g_full[1 - xl, z, at] = (x_recv[q, 0].astype(F32) + x_recv[q, 2].astype(F32)).astype(BF16)
        zg[q].start(1, 1)

    def left_split():
        load_l.wait()
        split_bf(in_bf.at[1], l_split)
        l_rows[xl] = l_split[xl]
        return send(l_split.at[1 - xl], l_rows.at[xl], k.at(dxl=1))

    def moments_split():
        for n in range(2):
            load_m[n].wait()
            for b in range(2):
                for t in range(8):
                    mom[n, b, :, pl.ds(t * 128, 128)] = mom_in[
                        n, pl.ds(t * 2 + b, 64, stride=16), :
                    ]
        return send(mom.at[:, 1 - xl], mom_recv, k.at(dxl=1))

    def left_columns():
        low = lax.broadcasted_iota(jnp.int32, (64, 128), 1) < 64
        for j in range(2):
            for zz in range(8):
                a = l_rows[j, :, pl.ds(zz // 2 * 128, 128)].astype(F32)
                b = l_rows[j, :, pl.ds((4 + zz // 2) * 128, 128)].astype(F32)
                if zz % 2:
                    a = pltpu.roll(a, 64, 1)
                else:
                    b = pltpu.roll(b, 64, 1)
                l_perm[zz, j] = jnp.where(low, a, b).astype(BF16)
        l_all[:, z] = l_perm[z]

    xt = left_split()
    core_sum(0)
    xq.wait_recv()
    zq.start(1, 1)
    zq.step(1, 0)
    y_pass(0)
    core_sum(1)
    xt.wait_recv()
    left_columns()
    zq.step(1, 1)
    y_sum(0)
    zq.step(2, 0)
    y_pass(1)
    zq.step(2, 1)
    x_sum(0)
    zq.step(3, 0)
    y_sum(1)
    zq.step(3, 1)
    zg[0].steps(1)
    x_sum(1)
    xm = moments_split()
    zg[0].steps(2)
    zg[1].steps(1)
    zg[0].steps(3)
    zg[1].steps(2)
    zg[0].steps(4)
    zg[1].steps(3)
    l_copies = [send(l_perm.at[lax.rem(z + o, 8)], l_all.at[:, z], k.at(dz=o)) for o in range(1, 8)]
    zq.steps(4)
    zg[1].steps(4)

    def dot(a, b):
        return jnp.dot(a, b, preferred_element_type=F32)

    left = l_rows[...].reshape(128, 1024)
    for t in range(4):
        cols = pl.ds(t * 256, 256)
        y_rot[:, cols] = dot(left, g_full[:, :, :, cols].reshape(1024, 256)).astype(BF16)
    xm.wait_recv()
    for t in range(4):
        cols = pl.ds(t * 256, 256)
        r = dot(y_rot[...], q_full[:, :, :, cols].reshape(1024, 256)).reshape(2, 64, 256)
        r_buf[:, :, cols] = r
        for j in range(2):
            first = mom[0, xl, :, cols] if j == 0 else mom_recv[0, :, cols]
            second = mom[1, xl, :, cols] if j == 0 else mom_recv[1, :, cols]
            rj = r_buf[lax.rem(xl + j, 2), :, cols]
            first = 0.9 * first + 0.1 * rj
            second = 0.95 * second + 0.05 * rj * rj
            n_buf[lax.rem(xl + j, 2), :, cols] = (first / (jnp.sqrt(second) + 1e-8)).astype(BF16)
    normal = n_buf[...].reshape(128, 1024)
    for h in range(H):
        slabs = q_full[...].reshape(1024, 1024)[h * W : (h + 1) * W]
        part = lax.dot_general(normal, slabs, CONTRACT_LAST, preferred_element_type=F32)
        part = part.astype(BF16).reshape(2, 64, W)
        for j in range(2):
            m_full[h, j, z] = part[j]
        if h < 2:
            zm[h].start(1, 0)
            zm[h].start(1, 1)

    xr = send(r_buf.at[1 - xl], r_recv, k.at(dxl=1))

    def left_gram():
        rows = g_full[:, z].reshape(128, 1024)
        for t in range(4):
            slabs = g_full[...].reshape(1024, 1024)[t * 256 : (t + 1) * 256]
            part = lax.dot_general(rows, slabs, CONTRACT_LAST, preferred_element_type=F32)
            pl_buf[:, :, pl.ds(t * 256, 256)] = part.reshape(2, 64, 256)

    def right_gram():
        half = lax.div(z, 2)
        odd = lax.rem(z, 2) == 1
        wide = lax.broadcasted_iota(jnp.int32, (128, 128), 1) < 64

        for j in range(2):
            for n in range(4):
                at = pl.ds(n * 2, 2)
                a = g_full[j, at, :, pl.ds(pl.multiple_of(half * 128, 128), 128)]
                b = g_full[j, at, :, pl.ds(pl.multiple_of((half + 4) * 128, 128), 128)]
                a, b = a.reshape(128, 128).astype(F32), b.reshape(128, 128).astype(F32)
                a = jnp.where(odd, pltpu.roll(a, 64, 1), a)
                b = jnp.where(odd, b, pltpu.roll(b, 64, 1))
                g_cols[:, pl.ds((j * 4 + n) * 128, 128)] = jnp.where(wide, a, b).T.astype(BF16)
        cols = g_cols[...]
        for t in range(4):
            at = pl.ds(t * 256, 256)
            pr_buf[:, :, at] = dot(cols, g_full[:, :, :, at].reshape(1024, 256)).reshape(2, 64, 256)

    up_copies = {}
    left_t = l_t

    def update(h):
        for t in range(W // 256):
            cols = pl.ds(t * 256, 256)
            part = dot(left_t[...], m_full[h, :, :, :, cols].reshape(1024, 256))
            up_send[h, :, :, cols] = part.astype(BF16).reshape(2, 64, 256)
        up_copies[h] = send(up_send.at[h, 1 - xl], up_recv.at[h], k.at(dxl=1))

    gathers = []

    class Gather:
        def __init__(self, h):
            self.h, self.got = h, {}

        def place(self, dy, dxh, dc, half=None):
            yy, hh, cc = lax.rem(y + dy, 4), lax.rem(xh + dxh, 2), lax.rem(c + dc, 2)
            ref = out.at[(yy * 2 + hh) * 2 + cc, self.h]
            if half is not None:
                ref = ref.at[pl.ds(half * (PIECE // 2), PIECE // 2)]
            return ref

        def push(self, name, src, peer, half=None):
            dst = src
            if src is None:
                src, dst = up_piece.at[self.h], self.place(0, 0, 0)
            self.got[name] = send(src, dst, peer)

        def begin(self):
            self.keep = local(up_piece.at[self.h], self.place(0, 0, 0))
            self.push("x", None, k.at(dxh=1))
            self.push((0, 1), None, k.at(dy=1))
            self.push((0, 3), None, k.at(dy=3))
            self.push((0, 0, "c"), None, k.at(dc=1))

        def x_arrive(self):
            self.got["x"].wait_recv()
            at = self.place(0, 1, 0)
            self.push((1, 1), at, k.at(dy=1))
            self.push((1, 3), at, k.at(dy=3))
            self.push((1, 0, "c"), at, k.at(dc=1))

        def relay(self, e):
            self.got[e, 1].wait_recv()
            self.push((e, 2, 0), self.place(3, e, 0, 0), k.at(dy=1))
            self.push((e, 1, "c"), self.place(3, e, 0), k.at(dc=1))
            self.got[e, 3].wait_recv()
            self.push((e, 2, 1), self.place(1, e, 0, 1), k.at(dy=3))
            self.push((e, 3, "c"), self.place(1, e, 0), k.at(dc=1))

        def finish(self, e):
            self.got[e, 2, 0].wait_recv()
            self.got[e, 2, 1].wait_recv()
            self.push((e, 2, "c"), self.place(2, e, 0), k.at(dc=1))

        def end(self):
            for e in range(2):
                for o in range(4):
                    self.got[e, o, "c"].wait_recv()
            self.keep.wait()

    gathers = [Gather(h) for h in range(H)]

    def pack_up(h):
        up_copies[h].wait_recv()
        n = W // 128
        for b in range(2):
            for t in range(n):
                cols = pl.ds(t * 128, 128)
                mine, theirs = up_send[h, xl, :, cols], up_recv[h, :, cols]
                piece = jnp.where(xl == b, mine.astype(F32), theirs.astype(F32))
                pack[pl.ds(t * 2 + b, 64, stride=2 * n), :] = piece
        up_piece[h] = pack[...].astype(BF16)
        gathers[h].begin()

    def woven(buf, received, b, t):
        cols = pl.ds(t * 128, 128)
        return jnp.where(xl == b, buf[xl, :, cols], received[:, cols])

    def new_moments():
        for b in range(2):
            for t in range(8):
                at = pl.ds(t * 2 + b, 64, stride=16)
                r = woven(r_buf, r_recv, b, t)
                new_first[at, :] = 0.9 * mom_in[0, at, :] + 0.1 * r
                new_second[at, :] = 0.95 * mom_in[1, at, :] + 0.05 * r * r

    def new_gram(dst, n, buf, received):
        load_g[n].wait()
        for b in range(2):
            for t in range(8):
                at = pl.ds(t * 2 + b, 64, stride=16)
                dst[at, :] = 0.95 * gram_in[n, at, :] + 0.05 * woven(buf, received, b, t)

    left_gram()
    xl_copy = send(pl_buf.at[1 - xl], pl_recv, k.at(dxl=1))
    zm[0].steps(1)
    zm[2].start(1, 0)
    zm[2].start(1, 1)
    zm[1].steps(1)
    zm[3].start(1, 0)
    zm[3].start(1, 1)
    right_gram()
    xr_copy = send(pr_buf.at[1 - xl], pr_recv, k.at(dxl=1))
    zm[0].steps(2)
    zm[2].steps(1)
    zm[1].steps(2)
    zm[3].steps(1)
    for copy in l_copies:
        copy.wait_recv()
    l_t[...] = l_all[...].reshape(1024, 128).astype(F32).T.astype(BF16)
    zm[0].steps(3)
    zm[2].steps(2)
    zm[1].steps(3)
    zm[3].steps(2)
    zm[0].steps(4)
    update(0)
    zm[2].steps(3)
    zm[1].steps(4)
    update(1)
    pack_up(0)
    zm[3].steps(3)
    zm[2].steps(4)
    update(2)
    pack_up(1)
    zm[3].steps(4)
    update(3)
    gathers[0].x_arrive()
    gathers[0].relay(0)
    pack_up(2)
    gathers[1].x_arrive()
    gathers[1].relay(0)
    pack_up(3)
    xr.wait_recv()
    new_moments()
    results = [local(new_first, new_first_out), local(new_second, new_second_out)]
    gathers[0].finish(0)
    gathers[0].relay(1)
    gathers[2].x_arrive()
    gathers[2].relay(0)
    gathers[1].finish(0)
    gathers[1].relay(1)
    gathers[3].x_arrive()
    gathers[3].relay(0)
    xl_copy.wait_recv()
    new_gram(new_left, 0, pl_buf, pl_recv)
    results.append(local(new_left, new_left_out))
    gathers[0].finish(1)
    gathers[2].finish(0)
    gathers[2].relay(1)
    gathers[1].finish(1)
    xr_copy.wait_recv()
    new_gram(new_right, 1, pr_buf, pr_recv)
    results.append(local(new_right, new_right_out))
    gathers[3].finish(0)
    gathers[3].relay(1)
    gathers[2].finish(1)
    gathers[3].finish(1)
    for gather in gathers:
        gather.end()
    for copy in results:
        copy.wait()
    for copy in unsent:
        copy.wait_send()


def write_out(part, n1, n2, nl, nr, update, o1, o2, ol, orr, held, whole, rest, sems):
    loads, copies = [], []
    top = lax.broadcasted_iota(jnp.int32, (8, 8, 128), 1) < 4
    for n in range(4):
        at = pl.ds(n * 4, 4)
        loads.append(pltpu.make_async_copy(part.at[at], held.at[at], sems.at[n]))
        loads[-1].start()
    for n, src in enumerate((n1, n2, nl, nr)):
        loads.append(pltpu.make_async_copy(src, rest.at[n], sems.at[4 + n]))
        loads[-1].start()
    for n in range(4):
        loads[n].wait()

        @pl.loop(n * 4, n * 4 + 4)
        def _(d):
            for r in range(4):
                a0, a1, a2, a3 = (
                    held[d, h, pl.ds(r * 64, 64), :].astype(F32).reshape(8, 8, 128)
                    for h in range(H)
                )
                even, odd = [], []
                for p, q in ((a0, a1), (a2, a3)):
                    even.append(jnp.where(top, p, pltpu.roll(q, 4, 1)))
                    odd.append(jnp.where(top, pltpu.roll(p, 4, 1), q))
                rows = jnp.stack([jnp.concatenate(even, axis=1), jnp.concatenate(odd, axis=1)], axis=1)
                whole[pl.ds(r * 16, 16), d] = rows.reshape(16, 16, 128).astype(BF16)

        at = (slice(None), pl.ds(n * 4, 4))
        copies.append(pltpu.make_async_copy(whole.at[at], update.at[at], sems.at[8 + n]))
        copies[-1].start()
    for n, dst in enumerate((o1, o2, ol, orr)):
        loads[4 + n].wait()
        copies.append(pltpu.make_async_copy(rest.at[n], dst, sems.at[n]))
        copies[-1].start()
    for copy in copies:
        copy.wait()


def per_device(grads, left_basis_t, right_basis, first, second, left_gram, right_gram):
    g = rows_view(grads[0]).reshape(64, 8, 2, 16, 128)
    lt, qr = (rows_view(a).reshape(64, 16, 128) for a in (left_basis_t, right_basis))
    m1, m2, lg, rg = (rows_view(a).reshape(1024, 128) for a in (first, second, left_gram, right_gram))
    hbm = pl.BlockSpec(memory_space=pl.ANY)
    shape = jax.ShapeDtypeStruct
    v = pltpu.VMEM
    done = pl.pallas_call(
        kernel,
        out_shape=[shape((16, H, PIECE, 128), BF16)] + [shape((1024, 128), F32)] * 4,
        in_specs=[hbm] * 7,
        out_specs=[hbm] * 5,
        scratch_shapes=[
            v((1024, 128), F32),
            v((1024, 128), F32),
            v((1024, 128), F32),
            v((1024, 128), F32),
            v((2, 1024, 128), F32),
            v((2, 64, 16, 128), BF16),
            v((2, 1024, 128), F32),
            v((2, 32, 8, 16, 128), BF16),
            v((2, 32, 8, 16, 128), BF16),
            v((2, 4, 2, 32, 16, 128), BF16),
            v((2, 2, 2, 32, 16, 128), BF16),
            v((2, 2, 32, 16, 128), BF16),
            v((2, 2, 2, 32, 1024), BF16),
            v((2, 3, 32, 1024), BF16),
            v((1024, 128), F32),
            v((2, 64, 1024), BF16),
            v((2, 8, 64, 1024), BF16),
            v((2, 64, 1024), BF16),
            v((2, 64, 1024), BF16),
            v((8, 2, 64, 128), BF16),
            v((2, 8, 64, 128), BF16),
            v((128, 1024), BF16),
            v((2, 8, 64, 1024), BF16),
            v((2, 2, 64, 1024), F32),
            v((2, 64, 1024), F32),
            v((128, 1024), BF16),
            v((2, 64, 1024), BF16),
            v((H, 2, 8, 64, W), BF16),
            v((2, 64, 1024), F32),
            v((64, 1024), F32),
            v((2, 64, 1024), F32),
            v((64, 1024), F32),
            v((2, 64, 1024), F32),
            v((64, 1024), F32),
            v((128, 1024), BF16),
            v((H, 2, 64, W), BF16),
            v((H, 64, W), BF16),
            v((PIECE, 128), F32),
            v((H, PIECE, 128), BF16),
            pltpu.SemaphoreType.DMA((NCOPY,)),
            pltpu.SemaphoreType.DMA((NCOPY,)),
            pltpu.SemaphoreType.DMA((16,)),
        ],
        compiler_params=pltpu.CompilerParams(
            collective_id=0, has_side_effects=True, vmem_limit_bytes=56 << 20
        ),
        name="soap",
    )(g, lt, qr, m1, m2, lg, rg)
    update, *rest = pl.pallas_call(
        write_out,
        out_shape=[shape((64, 16, 16, 128), BF16)] + [shape((1024, 128), F32)] * 4,
        in_specs=[hbm] * 5,
        out_specs=[hbm] * 5,
        scratch_shapes=[
            v((16, H, PIECE, 128), BF16),
            v((64, 16, 16, 128), BF16),
            v((4, 1024, 128), F32),
            pltpu.SemaphoreType.DMA((12,)),
        ],
        compiler_params=pltpu.CompilerParams(vmem_limit_bytes=56 << 20),
        name="write_out",
    )(*done)
    update = update.reshape(64, 128, 2, 128).transpose(0, 2, 1, 3).reshape(64, 2, 16384)

    def back(a):
        return a.reshape(64, 8, 2, 128).transpose(0, 2, 1, 3).reshape(64, 2, 1024)

    return (update, *(back(a) for a in rest))


def solution(mesh):
    sharded = P("fsdp", None, "dp")
    return jax.shard_map(
        per_device,
        mesh=mesh,
        in_specs=(P("dp", "fsdp", None, None),) + (sharded,) * 6,
        out_specs=(P("fsdp", None, None),) + (sharded,) * 4,
        check_vma=False,
    )
```

```python
import jax
import jax.numpy as jnp
from jax import lax
from jax.experimental import pallas as pl
from jax.experimental.pallas import tpu as pltpu
from jax.sharding import PartitionSpec as P

MESH = pl.DeviceIdType.MESH
F32, BF16 = jnp.float32, jnp.bfloat16
NCOPY = 256
H = 4
W = 1024 // H
PIECE = 1024 // H
CONTRACT_LAST = (((1,), (1,)), ((), ()))


def rows_view(x):
    i, b, n = x.shape
    return x.reshape(i, b, n // 128, 128).transpose(0, 2, 1, 3)


class Peers:
    def __init__(self):
        dp, fs = lax.axis_index("dp"), lax.axis_index("fsdp")
        self.y, self.xh, self.c = lax.div(dp, 4), lax.rem(lax.div(dp, 2), 2), lax.rem(dp, 2)
        self.xl, self.z = lax.div(fs, 8), lax.rem(fs, 8)

    def at(self, dy=0, dxh=0, dc=0, dxl=0, dz=0):
        y, xh, c = lax.rem(self.y + dy, 4), lax.rem(self.xh + dxh, 2), lax.rem(self.c + dc, 2)
        xl, z = lax.rem(self.xl + dxl, 2), lax.rem(self.z + dz, 8)
        return ((y * 2 + xh) * 2 + c, xl * 8 + z)


def kernel(
    g, lt, qr, m1, m2, lg, rg,
    out, new_first_out, new_second_out, new_left_out, new_right_out,
    new_first, new_second, new_left, new_right, gram_in, in_bf, mom_in, own, other, summed, y_recv, y_relay, x_send, x_recv, acc,
    q_split, q_full, l_split, l_rows, l_perm, l_all, l_t,
    g_full, mom, mom_recv, y_rot, n_buf, m_full, r_buf, r_recv, pl_buf, pl_recv, pr_buf, pr_recv,
    ret, g_cols, up_send, up_recv, pack, up_piece,
    ss, rs, ls,
):
    k = Peers()
    y, xh, c, xl, z = k.y, k.xh, k.c, k.xl, k.z
    count = [0, 0]
    unsent = []

    def remote(src, dst, peer):
        n = count[0]
        count[0] += 1
        copy = pltpu.make_async_remote_copy(
            src, dst, ss.at[n], rs.at[n], device_id=peer, device_id_type=MESH
        )
        unsent.append(copy)
        return copy

    def send(src, dst, peer):
        copy = remote(src, dst, peer)
        copy.start()
        return copy

    def local(src, dst):
        n = count[1]
        count[1] += 1
        copy = pltpu.make_async_copy(src, dst, ls.at[n])
        copy.start()
        return copy

    partners = (
        [k.at(dc=1), k.at(dxl=1), k.at(dxh=1), k.at(dxh=1, dxl=1)]
        + [k.at(dy=o) for o in (1, 2, 3)]
        + [k.at(dz=o) for o in range(1, 8)]
    )
    barrier = pltpu.get_barrier_semaphore()
    for peer in partners:
        pl.semaphore_signal(barrier, inc=1, device_id=peer, device_id_type=MESH)

    load_q = local(qr, in_bf.at[0])
    load_l = local(lt, in_bf.at[1])
    def pairs(q, o):
        two = pl.ds(lax.rem(y + o, 4) * 2, 2)
        rows = pl.ds(q * 32, 32)
        return [g.at[rows, two, cc] for cc in (c, 1 - c)], (q, slice(None), two)

    def load_pair(q, o):
        (mine, _), at = pairs(q, o)
        return local(mine, own.at[at])

    def swap_pair(q, o):
        (_, theirs), at = pairs(q, o)
        return send(theirs, other.at[at], k.at(dc=1))

    order = (2, 1, 3, 0)
    load_own = {(q, o): load_pair(q, o) for q in range(2) for o in order}
    load_m = [local(m1, mom_in.at[0]), local(m2, mom_in.at[1])]
    load_g = [local(lg, gram_in.at[0]), local(rg, gram_in.at[1])]

    def split_bf(src, dst):
        acc[...] = src[...].reshape(1024, 128).astype(F32)
        for b in range(2):
            for t in range(8):
                dst[b, :, pl.ds(t * 128, 128)] = acc[pl.ds(t * 2 + b, 64, stride=16), :].astype(BF16)

    class ZGather:
        def __init__(self, ref, skip=False):
            self.ref, self.copies, self.skip = ref, {}, skip

        def start(self, s, j):
            for d in (1, -1):
                if s == 4 and j != (d == -1):
                    continue
                back, on = (2, 2) if s == 4 and self.skip else (s - 1, 1)
                at = self.ref(lax.rem(xl + j, 2), lax.rem(z - d * back + 8, 8))
                self.copies[s, j, d] = send(at, at, k.at(dz=d * on % 8))

        def arrive(self, s, j):
            for d in (1, -1):
                if (s, j, d) in self.copies:
                    self.copies[s, j, d].wait_recv()

        def step(self, s, j):
            self.arrive(s, j)
            if s < 3 or s == 3 and not self.skip:
                self.start(s + 1, j)
            if s == 2 and self.skip:
                self.start(4, j)

        def steps(self, s):
            self.step(s, 0)
            self.step(s, 1)

    zq = ZGather(lambda j, zz: q_full.at[j, zz])
    zg = [
        ZGather(lambda j, zz, q=q: g_full.at[j, zz, pl.ds(q * 32, 32), :], q == 1) for q in range(2)
    ]
    zm = [ZGather(lambda j, zz, h=h: m_full.at[h, j, zz], False) for h in range(H)]

    def left_columns(j):
        low = lax.broadcasted_iota(jnp.int32, (64, 128), 1) < 64
        for zz in range(8):
            a = l_rows[j, :, pl.ds(zz // 2 * 128, 128)].astype(F32)
            b = l_rows[j, :, pl.ds((4 + zz // 2) * 128, 128)].astype(F32)
            if zz % 2:
                a = pltpu.roll(a, 64, 1)
            else:
                b = pltpu.roll(b, 64, 1)
            l_perm[zz, j] = jnp.where(low, a, b).astype(BF16)
        l_all[j, z] = l_perm[z, j]

    def left_send(j):
        return [
            send(l_perm.at[lax.rem(z + o, 8), j], l_all.at[j, z], k.at(dz=o))
            for o in (1, 7, 2, 6, 3, 5, 4)
        ]

    load_q.wait()
    split_bf(in_bf.at[0], q_split)
    q_full[xl, z] = q_split[xl]
    load_l.wait()
    split_bf(in_bf.at[1], l_split)
    l_rows[xl] = l_split[xl]
    left_columns(xl)
    pl.semaphore_wait(barrier, len(partners))
    core = {(0, o): swap_pair(0, o) for o in order}
    zq.start(1, 0)
    xq = send(q_split.at[1 - xl], q_full.at[xl, z], k.at(dxl=1))
    xt = send(l_split.at[1 - xl], l_rows.at[xl], k.at(dxl=1))
    l_copies = left_send(xl)
    y_copies = {}

    def core_sum(q):
        for o in order:
            load_own[q, o].wait()
            core[q, o].wait_recv()
            yy = lax.rem(y + o, 4)

            @pl.loop(0, 8)
            def _(i):
                at = (q, pl.ds(i * 4, 4), pl.ds(yy * 2, 2))
                total = (own[at].astype(F32) + other[at].astype(F32)).astype(BF16)
                for e in range(2):
                    summed[q, yy, e, pl.ds(i * 4, 4)] = total[:, e]

            if o == 2:
                y_copies[q, "far", 1] = send(summed.at[q, yy, 0], y_relay.at[q, 0], k.at(dy=1))
                y_copies[q, "far", 3] = send(summed.at[q, yy, 1], y_relay.at[q, 1], k.at(dy=3))
            elif o:
                e = 1 if o == 1 else 0
                y_copies[q, "near", o] = send(
                    summed.at[q, yy, e], y_recv.at[q, o // 2, e], k.at(dy=o)
                )

    def y_pass(q):
        for e, o in ((0, 1), (1, 3)):
            y_copies[q, "far", o].wait_recv()
            yy = lax.rem(y + o, 4)

            @pl.loop(0, 4)
            def _(i):
                at = pl.ds(i * 8, 8)
                total = summed[q, yy, e, at].astype(F32) + y_relay[q, e, at].astype(F32)
                y_relay[q, e, at] = total.astype(BF16)

            y_copies[q, "sum", o] = send(y_relay.at[q, e], y_recv.at[q, o // 2, e], k.at(dy=o))

    x_copies = {}

    def y_sum(q):
        for o in (1, 3):
            y_copies[q, "near", o].wait_recv()
            y_copies[q, "sum", o].wait_recv()
        for e in range(2):

            @pl.loop(0, 4)
            def _(i):
                at = pl.ds(i * 8, 8)
                total = summed[q, y, e, at].astype(F32)
                for o in range(2):
                    total += y_recv[q, o, e, at].astype(F32)
                acc[pl.ds(e * 512 + i * 128, 128), :] = total.reshape(128, 128)

            for b in range(2):
                for t in range(8):
                    x_send[q, e, b, :, pl.ds(t * 128, 128)] = acc[
                        pl.ds(e * 512 + t * 2 + b, 32, stride=16), :
                    ].astype(BF16)
        for n, (dh, dl) in enumerate(((1, 1), (1, 0), (0, 1))):
            x_copies[q, n] = send(
                x_send.at[q, lax.rem(xh + dh, 2), lax.rem(xl + dl, 2)],
                x_recv.at[q, n],
                k.at(dxh=dh, dxl=dl),
            )

    def x_sum(q):
        at = pl.ds(q * 32, 32)
        x_copies[q, 1].wait_recv()
        g_full[xl, z, at] = (
            x_send[q, xh, xl].astype(F32) + x_recv[q, 1].astype(F32)
        ).astype(BF16)
        zg[q].start(1, 0)
        x_copies[q, 0].wait_recv()
        x_copies[q, 2].wait_recv()
        g_full[1 - xl, z, at] = (x_recv[q, 0].astype(F32) + x_recv[q, 2].astype(F32)).astype(BF16)
        zg[q].start(1, 1)

    def moments_split():
        for n in range(2):
            load_m[n].wait()
            for b in range(2):
                for t in range(8):
                    mom[n, b, :, pl.ds(t * 128, 128)] = mom_in[
                        n, pl.ds(t * 2 + b, 64, stride=16), :
                    ]
        return send(mom.at[:, 1 - xl], mom_recv, k.at(dxl=1))

    core_sum(0)
    core.update({(1, o): swap_pair(1, o) for o in order})
    xq.wait_recv()
    zq.start(1, 1)
    zq.step(1, 0)
    y_pass(0)
    core_sum(1)
    xt.wait_recv()
    left_columns(1 - xl)
    zq.step(1, 1)
    y_sum(0)
    zq.step(2, 0)
    y_pass(1)
    zq.step(2, 1)
    x_sum(0)
    zq.step(3, 0)
    y_sum(1)
    zq.step(3, 1)
    zg[0].steps(1)
    x_sum(1)
    xm = moments_split()
    zg[0].steps(2)
    zg[1].steps(1)
    zg[0].steps(3)
    zg[1].steps(2)
    zg[0].steps(4)
    zg[1].steps(3)
    l_copies += left_send(1 - xl)
    zq.steps(4)
    zg[1].steps(4)

    def dot(a, b):
        return jnp.dot(a, b, preferred_element_type=F32)

    left = l_rows[...].reshape(128, 1024)
    for t in range(4):
        cols = pl.ds(t * 256, 256)
        y_rot[:, cols] = dot(left, g_full[:, :, :, cols].reshape(1024, 256)).astype(BF16)
    xm.wait_recv()
    for t in range(4):
        cols = pl.ds(t * 256, 256)
        r = dot(y_rot[...], q_full[:, :, :, cols].reshape(1024, 256)).reshape(2, 64, 256)
        r_buf[:, :, cols] = r
        for j in range(2):
            first = mom[0, xl, :, cols] if j == 0 else mom_recv[0, :, cols]
            second = mom[1, xl, :, cols] if j == 0 else mom_recv[1, :, cols]
            rj = r_buf[lax.rem(xl + j, 2), :, cols]
            first = 0.9 * first + 0.1 * rj
            second = 0.95 * second + 0.05 * rj * rj
            n_buf[lax.rem(xl + j, 2), :, cols] = (first / (jnp.sqrt(second) + 1e-8)).astype(BF16)
    normal = n_buf[...].reshape(128, 1024)
    for h in range(H):
        slabs = q_full[...].reshape(1024, 1024)[h * W : (h + 1) * W]
        part = lax.dot_general(normal, slabs, CONTRACT_LAST, preferred_element_type=F32)
        part = part.astype(BF16).reshape(2, 64, W)
        for j in range(2):
            m_full[h, j, z] = part[j]
        if h < 2:
            zm[h].start(1, 0)
            zm[h].start(1, 1)

    ret[0] = r_buf[1 - xl].astype(BF16)
    xr = send(ret.at[0], r_recv, k.at(dxl=1))

    def left_gram():
        rows = g_full[:, z].reshape(128, 1024)
        for t in range(4):
            slabs = g_full[...].reshape(1024, 1024)[t * 256 : (t + 1) * 256]
            part = lax.dot_general(rows, slabs, CONTRACT_LAST, preferred_element_type=F32)
            pl_buf[:, :, pl.ds(t * 256, 256)] = part.reshape(2, 64, 256)

    def right_gram():
        half = lax.div(z, 2)
        odd = lax.rem(z, 2) == 1
        wide = lax.broadcasted_iota(jnp.int32, (128, 128), 1) < 64

        for j in range(2):
            for n in range(4):
                at = pl.ds(n * 2, 2)
                a = g_full[j, at, :, pl.ds(pl.multiple_of(half * 128, 128), 128)]
                b = g_full[j, at, :, pl.ds(pl.multiple_of((half + 4) * 128, 128), 128)]
                a, b = a.reshape(128, 128).astype(F32), b.reshape(128, 128).astype(F32)
                a = jnp.where(odd, pltpu.roll(a, 64, 1), a)
                b = jnp.where(odd, b, pltpu.roll(b, 64, 1))
                g_cols[:, pl.ds((j * 4 + n) * 128, 128)] = jnp.where(wide, a, b).T.astype(BF16)
        cols = g_cols[...]
        for t in range(4):
            at = pl.ds(t * 256, 256)
            pr_buf[:, :, at] = dot(cols, g_full[:, :, :, at].reshape(1024, 256)).reshape(2, 64, 256)

    up_copies = {}
    left_t = l_t

    def update(h):
        for t in range(W // 256):
            cols = pl.ds(t * 256, 256)
            part = dot(left_t[...], m_full[h, :, :, :, cols].reshape(1024, 256))
            up_send[h, :, :, cols] = part.astype(BF16).reshape(2, 64, 256)
        up_copies[h] = send(up_send.at[h, 1 - xl], up_recv.at[h], k.at(dxl=1))

    gathers = []

    class Gather:
        def __init__(self, h):
            self.h, self.got = h, {}

        def place(self, dy, dxh, dc, half=None):
            yy, hh, cc = lax.rem(y + dy, 4), lax.rem(xh + dxh, 2), lax.rem(c + dc, 2)
            ref = out.at[(yy * 2 + hh) * 2 + cc, self.h]
            if half is not None:
                ref = ref.at[pl.ds(half * (PIECE // 2), PIECE // 2)]
            return ref

        def push(self, name, src, peer, half=None):
            dst = src
            if src is None:
                src, dst = up_piece.at[self.h], self.place(0, 0, 0)
            self.got[name] = send(src, dst, peer)

        def begin(self):
            self.keep = local(up_piece.at[self.h], self.place(0, 0, 0))
            self.push("x", None, k.at(dxh=1))
            self.push((0, 1), None, k.at(dy=1))
            self.push((0, 3), None, k.at(dy=3))
            self.push((0, 0, "c"), None, k.at(dc=1))

        def x_arrive(self):
            self.got["x"].wait_recv()
            at = self.place(0, 1, 0)
            self.push((1, 1), at, k.at(dy=1))
            self.push((1, 3), at, k.at(dy=3))
            self.push((1, 0, "c"), at, k.at(dc=1))

        def relay(self, e):
            self.got[e, 1].wait_recv()
            self.push((e, 2, 0), self.place(3, e, 0, 0), k.at(dy=1))
            self.push((e, 1, "c"), self.place(3, e, 0), k.at(dc=1))
            self.got[e, 3].wait_recv()
            self.push((e, 2, 1), self.place(1, e, 0, 1), k.at(dy=3))
            self.push((e, 3, "c"), self.place(1, e, 0), k.at(dc=1))

        def finish(self, e):
            self.got[e, 2, 0].wait_recv()
            self.got[e, 2, 1].wait_recv()
            self.push((e, 2, "c"), self.place(2, e, 0), k.at(dc=1))

        def end(self):
            for e in range(2):
                for o in range(4):
                    self.got[e, o, "c"].wait_recv()
            self.keep.wait()

    class GatherYFirst(Gather):
        def begin(self):
            self.keep = local(up_piece.at[self.h], self.place(0, 0, 0))
            self.push((0, 1), None, k.at(dy=1))
            self.push((0, 3), None, k.at(dy=3))
            self.push((0, "x"), None, k.at(dxh=1))
            self.push((0, 0, "c"), None, k.at(dc=1))

        def relay(self, e):
            for o, half in ((1, 0), (3, 1)):
                self.got[0, o].wait_recv()
                self.push((0, 2, half), self.place(4 - o, 0, 0, half), k.at(dy=o))
                self.push((o, "x"), self.place(4 - o, 0, 0), k.at(dxh=1))
                self.push((0, o, "c"), self.place(4 - o, 0, 0), k.at(dc=1))

        def finish(self, e):
            for half in range(2):
                self.got[0, 2, half].wait_recv()
            self.push((2, "x"), self.place(2, 0, 0), k.at(dxh=1))
            self.push((0, 2, "c"), self.place(2, 0, 0), k.at(dc=1))

        def x_arrive(self, steps):
            for o in steps:
                self.got[o, "x"].wait_recv()
                self.push((1, o, "c"), self.place(4 - o if o else 0, 1, 0), k.at(dc=1))

    gathers = [GatherYFirst(0)] + [Gather(h) for h in range(1, H)]

    def pack_up(h):
        up_copies[h].wait_recv()
        n = W // 128
        for b in range(2):
            for t in range(n):
                cols = pl.ds(t * 128, 128)
                mine, theirs = up_send[h, xl, :, cols], up_recv[h, :, cols]
                piece = jnp.where(xl == b, mine.astype(F32), theirs.astype(F32))
                pack[pl.ds(t * 2 + b, 64, stride=2 * n), :] = piece
        up_piece[h] = pack[...].astype(BF16)
        gathers[h].begin()

    def woven(buf, received, b, t):
        cols = pl.ds(t * 128, 128)
        return jnp.where(xl == b, buf[xl, :, cols], received[:, cols].astype(F32))

    def new_moments():
        for b in range(2):
            for t in range(8):
                at = pl.ds(t * 2 + b, 64, stride=16)
                r = woven(r_buf, r_recv, b, t)
                new_first[at, :] = 0.9 * mom_in[0, at, :] + 0.1 * r
                new_second[at, :] = 0.95 * mom_in[1, at, :] + 0.05 * r * r

    def new_gram(dst, n, buf, received):
        load_g[n].wait()
        for b in range(2):
            for t in range(8):
                at = pl.ds(t * 2 + b, 64, stride=16)
                dst[at, :] = 0.95 * gram_in[n, at, :] + 0.05 * woven(buf, received, b, t)

    left_gram()
    ret[1] = pl_buf[1 - xl].astype(BF16)
    xl_copy = send(ret.at[1], pl_recv, k.at(dxl=1))
    zm[0].steps(1)
    zm[2].start(1, 0)
    zm[2].start(1, 1)
    zm[1].steps(1)
    zm[3].start(1, 0)
    zm[3].start(1, 1)
    right_gram()
    ret[2] = pr_buf[1 - xl].astype(BF16)
    xr_copy = send(ret.at[2], pr_recv, k.at(dxl=1))
    zm[0].steps(2)
    zm[2].steps(1)
    zm[1].steps(2)
    zm[3].steps(1)
    for copy in l_copies:
        copy.wait_recv()
    l_t[...] = l_all[...].reshape(1024, 128).astype(F32).T.astype(BF16)
    zm[0].steps(3)
    zm[2].steps(2)
    zm[1].steps(3)
    zm[3].steps(2)
    zm[0].steps(4)
    update(0)
    zm[2].steps(3)
    zm[1].steps(4)
    update(1)
    pack_up(0)
    zm[3].steps(3)
    zm[2].steps(4)
    update(2)
    pack_up(1)
    zm[3].steps(4)
    update(3)
    gathers[0].relay(0)
    pack_up(2)
    gathers[1].x_arrive()
    gathers[1].relay(0)
    pack_up(3)
    xr.wait_recv()
    new_moments()
    results = [local(new_first, new_first_out), local(new_second, new_second_out)]
    gathers[0].finish(0)
    gathers[0].x_arrive((0,))
    gathers[2].x_arrive()
    gathers[2].relay(0)
    gathers[1].finish(0)
    gathers[1].relay(1)
    gathers[3].x_arrive()
    gathers[3].relay(0)
    gathers[0].x_arrive((1, 3))
    xl_copy.wait_recv()
    new_gram(new_left, 0, pl_buf, pl_recv)
    results.append(local(new_left, new_left_out))
    gathers[2].finish(0)
    gathers[2].relay(1)
    gathers[1].finish(1)
    gathers[0].x_arrive((2,))
    xr_copy.wait_recv()
    new_gram(new_right, 1, pr_buf, pr_recv)
    results.append(local(new_right, new_right_out))
    gathers[3].finish(0)
    gathers[3].relay(1)
    gathers[2].finish(1)
    gathers[3].finish(1)
    for gather in gathers:
        gather.end()
    for copy in results:
        copy.wait()
    for copy in unsent:
        copy.wait_send()


def write_out(part, n1, n2, nl, nr, update, o1, o2, ol, orr, held, whole, rest, sems):
    loads, copies = [], []
    top = lax.broadcasted_iota(jnp.int32, (8, 8, 128), 1) < 4
    for n in range(4):
        at = pl.ds(n * 4, 4)
        loads.append(pltpu.make_async_copy(part.at[at], held.at[at], sems.at[n]))
        loads[-1].start()
    for n, src in enumerate((n1, n2, nl, nr)):
        loads.append(pltpu.make_async_copy(src, rest.at[n], sems.at[4 + n]))
        loads[-1].start()
    for n in range(4):
        loads[n].wait()

        @pl.loop(n * 4, n * 4 + 4)
        def _(d):
            for r in range(4):
                a0, a1, a2, a3 = (
                    held[d, h, pl.ds(r * 64, 64), :].astype(F32).reshape(8, 8, 128)
                    for h in range(H)
                )
                even, odd = [], []
                for p, q in ((a0, a1), (a2, a3)):
                    even.append(jnp.where(top, p, pltpu.roll(q, 4, 1)))
                    odd.append(jnp.where(top, pltpu.roll(p, 4, 1), q))
                rows = jnp.stack([jnp.concatenate(even, axis=1), jnp.concatenate(odd, axis=1)], axis=1)
                whole[pl.ds(r * 16, 16), d] = rows.reshape(16, 16, 128).astype(BF16)

        at = (slice(None), pl.ds(n * 4, 4))
        copies.append(pltpu.make_async_copy(whole.at[at], update.at[at], sems.at[8 + n]))
        copies[-1].start()
    for n, dst in enumerate((o1, o2, ol, orr)):
        loads[4 + n].wait()
        copies.append(pltpu.make_async_copy(rest.at[n], dst, sems.at[n]))
        copies[-1].start()
    for copy in copies:
        copy.wait()


def per_device(grads, left_basis_t, right_basis, first, second, left_gram, right_gram):
    g = rows_view(grads[0]).reshape(64, 8, 2, 16, 128)
    lt, qr = (rows_view(a).reshape(64, 16, 128) for a in (left_basis_t, right_basis))
    m1, m2, lg, rg = (rows_view(a).reshape(1024, 128) for a in (first, second, left_gram, right_gram))
    hbm = pl.BlockSpec(memory_space=pl.ANY)
    shape = jax.ShapeDtypeStruct
    v = pltpu.VMEM
    done = pl.pallas_call(
        kernel,
        out_shape=[shape((16, H, PIECE, 128), BF16)] + [shape((1024, 128), F32)] * 4,
        in_specs=[hbm] * 7,
        out_specs=[hbm] * 5,
        scratch_shapes=[
            v((1024, 128), F32),
            v((1024, 128), F32),
            v((1024, 128), F32),
            v((1024, 128), F32),
            v((2, 1024, 128), F32),
            v((2, 64, 16, 128), BF16),
            v((2, 1024, 128), F32),
            v((2, 32, 8, 16, 128), BF16),
            v((2, 32, 8, 16, 128), BF16),
            v((2, 4, 2, 32, 16, 128), BF16),
            v((2, 2, 2, 32, 16, 128), BF16),
            v((2, 2, 32, 16, 128), BF16),
            v((2, 2, 2, 32, 1024), BF16),
            v((2, 3, 32, 1024), BF16),
            v((1024, 128), F32),
            v((2, 64, 1024), BF16),
            v((2, 8, 64, 1024), BF16),
            v((2, 64, 1024), BF16),
            v((2, 64, 1024), BF16),
            v((8, 2, 64, 128), BF16),
            v((2, 8, 64, 128), BF16),
            v((128, 1024), BF16),
            v((2, 8, 64, 1024), BF16),
            v((2, 2, 64, 1024), F32),
            v((2, 64, 1024), F32),
            v((128, 1024), BF16),
            v((2, 64, 1024), BF16),
            v((H, 2, 8, 64, W), BF16),
            v((2, 64, 1024), F32),
            v((64, 1024), BF16),
            v((2, 64, 1024), F32),
            v((64, 1024), BF16),
            v((2, 64, 1024), F32),
            v((64, 1024), BF16),
            v((3, 64, 1024), BF16),
            v((128, 1024), BF16),
            v((H, 2, 64, W), BF16),
            v((H, 64, W), BF16),
            v((PIECE, 128), F32),
            v((H, PIECE, 128), BF16),
            pltpu.SemaphoreType.DMA((NCOPY,)),
            pltpu.SemaphoreType.DMA((NCOPY,)),
            pltpu.SemaphoreType.DMA((24,)),
        ],
        compiler_params=pltpu.CompilerParams(
            collective_id=0, has_side_effects=True, vmem_limit_bytes=56 << 20
        ),
        name="soap",
    )(g, lt, qr, m1, m2, lg, rg)
    update, *rest = pl.pallas_call(
        write_out,
        out_shape=[shape((64, 16, 16, 128), BF16)] + [shape((1024, 128), F32)] * 4,
        in_specs=[hbm] * 5,
        out_specs=[hbm] * 5,
        scratch_shapes=[
            v((16, H, PIECE, 128), BF16),
            v((64, 16, 16, 128), BF16),
            v((4, 1024, 128), F32),
            pltpu.SemaphoreType.DMA((12,)),
        ],
        compiler_params=pltpu.CompilerParams(vmem_limit_bytes=56 << 20),
        name="write_out",
    )(*done)
    update = update.reshape(64, 128, 2, 128).transpose(0, 2, 1, 3).reshape(64, 2, 16384)

    def back(a):
        return a.reshape(64, 8, 2, 128).transpose(0, 2, 1, 3).reshape(64, 2, 1024)

    return (update, *(back(a) for a in rest))


def solution(mesh):
    sharded = P("fsdp", None, "dp")
    return jax.shard_map(
        per_device,
        mesh=mesh,
        in_specs=(P("dp", "fsdp", None, None),) + (sharded,) * 6,
        out_specs=(P("fsdp", None, None),) + (sharded,) * 4,
        check_vma=False,
    )
```

```python
import jax
import jax.numpy as jnp
from jax import lax
from jax.experimental import pallas as pl
from jax.experimental.pallas import tpu as pltpu
from jax.sharding import PartitionSpec as P

MESH = pl.DeviceIdType.MESH
F32, BF16 = jnp.float32, jnp.bfloat16
NCOPY = 256
H = 4
W = 1024 // H
PIECE = 1024 // H
CONTRACT_LAST = (((1,), (1,)), ((), ()))


def rows_view(x):
    i, b, n = x.shape
    return x.reshape(i, b, n // 128, 128).transpose(0, 2, 1, 3)


class Peers:
    def __init__(self):
        dp, fs = lax.axis_index("dp"), lax.axis_index("fsdp")
        self.y, self.xh, self.c = lax.div(dp, 4), lax.rem(lax.div(dp, 2), 2), lax.rem(dp, 2)
        self.xl, self.z = lax.div(fs, 8), lax.rem(fs, 8)

    def at(self, dy=0, dxh=0, dc=0, dxl=0, dz=0):
        y, xh, c = lax.rem(self.y + dy, 4), lax.rem(self.xh + dxh, 2), lax.rem(self.c + dc, 2)
        xl, z = lax.rem(self.xl + dxl, 2), lax.rem(self.z + dz, 8)
        return ((y * 2 + xh) * 2 + c, xl * 8 + z)


def kernel(
    g, lt, qr, m1, m2, lg, rg,
    out, new_first_out, new_second_out, new_left_out, new_right_out,
    new_first, new_second, new_left, new_right, gram_in, in_bf, mom_in, own, other, summed, y_recv, y_relay, x_send, x_recv, acc,
    q_split, q_full, l_split, l_rows, l_perm, l_all, l_t,
    g_full, mom, mom_recv, y_rot, n_buf, m_full, r_buf, r_recv, pl_buf, pl_recv, pr_buf, pr_recv,
    ret, g_cols, up_send, up_recv, pack, up_piece,
    ss, rs, ls,
):
    k = Peers()
    y, xh, c, xl, z = k.y, k.xh, k.c, k.xl, k.z
    count = [0, 0]
    unsent = []

    def remote(src, dst, peer):
        n = count[0]
        count[0] += 1
        copy = pltpu.make_async_remote_copy(
            src, dst, ss.at[n], rs.at[n], device_id=peer, device_id_type=MESH
        )
        unsent.append(copy)
        return copy

    def send(src, dst, peer):
        copy = remote(src, dst, peer)
        copy.start()
        return copy

    def local(src, dst):
        n = count[1]
        count[1] += 1
        copy = pltpu.make_async_copy(src, dst, ls.at[n])
        copy.start()
        return copy

    partners = (
        [k.at(dc=1), k.at(dxl=1), k.at(dxh=1), k.at(dxh=1, dxl=1)]
        + [k.at(dy=o) for o in (1, 2, 3)]
        + [k.at(dz=o) for o in range(1, 8)]
    )
    barrier = pltpu.get_barrier_semaphore()
    for peer in partners:
        pl.semaphore_signal(barrier, inc=1, device_id=peer, device_id_type=MESH)

    load_q = local(qr, in_bf.at[0])
    load_l = local(lt, in_bf.at[1])
    def pairs(q, o):
        two = pl.ds(lax.rem(y + o, 4) * 2, 2)
        rows = pl.ds(q * 32, 32)
        return [g.at[rows, two, cc] for cc in (c, 1 - c)], (q, slice(None), two)

    def load_pair(q, o):
        (mine, _), at = pairs(q, o)
        return local(mine, own.at[at])

    def swap_pair(q, o):
        (_, theirs), at = pairs(q, o)
        return send(theirs, other.at[at], k.at(dc=1))

    order = (2, 1, 3, 0)
    load_own = {(q, o): load_pair(q, o) for q in range(2) for o in order}
    load_m = [local(m1, mom_in.at[0]), local(m2, mom_in.at[1])]
    load_g = [local(lg, gram_in.at[0]), local(rg, gram_in.at[1])]

    def split_bf(src, dst):
        acc[...] = src[...].reshape(1024, 128).astype(F32)
        for b in range(2):
            for t in range(8):
                dst[b, :, pl.ds(t * 128, 128)] = acc[pl.ds(t * 2 + b, 64, stride=16), :].astype(BF16)

    class ZGather:
        def __init__(self, ref, skip=False):
            self.ref, self.copies, self.skip = ref, {}, skip

        def start(self, s, j):
            for d in (1, -1):
                if s == 4 and j != (d == -1):
                    continue
                back, on = (2, 2) if s == 4 and self.skip else (s - 1, 1)
                at = self.ref(lax.rem(xl + j, 2), lax.rem(z - d * back + 8, 8))
                self.copies[s, j, d] = send(at, at, k.at(dz=d * on % 8))

        def arrive(self, s, j):
            for d in (1, -1):
                if (s, j, d) in self.copies:
                    self.copies[s, j, d].wait_recv()

        def step(self, s, j):
            self.arrive(s, j)
            if s < 3 or s == 3 and not self.skip:
                self.start(s + 1, j)
            if s == 2 and self.skip:
                self.start(4, j)

        def steps(self, s):
            self.step(s, 0)
            self.step(s, 1)

    zq = ZGather(lambda j, zz: q_full.at[j, zz])
    zg = [
        ZGather(lambda j, zz, q=q: g_full.at[j, zz, pl.ds(q * 32, 32), :], q == 1) for q in range(2)
    ]
    zm = [ZGather(lambda j, zz, h=h: m_full.at[h, j, zz], False) for h in range(H)]

    def left_columns(j):
        low = lax.broadcasted_iota(jnp.int32, (64, 128), 1) < 64
        for zz in range(8):
            a = l_rows[j, :, pl.ds(zz // 2 * 128, 128)].astype(F32)
            b = l_rows[j, :, pl.ds((4 + zz // 2) * 128, 128)].astype(F32)
            if zz % 2:
                a = pltpu.roll(a, 64, 1)
            else:
                b = pltpu.roll(b, 64, 1)
            l_perm[zz, j] = jnp.where(low, a, b).astype(BF16)
        l_all[j, z] = l_perm[z, j]

    def left_send(j):
        return [
            send(l_perm.at[lax.rem(z + o, 8), j], l_all.at[j, z], k.at(dz=o))
            for o in (1, 7, 2, 6, 3, 5, 4)
        ]

    load_q.wait()
    split_bf(in_bf.at[0], q_split)
    q_full[xl, z] = q_split[xl]
    load_l.wait()
    split_bf(in_bf.at[1], l_split)
    l_rows[xl] = l_split[xl]
    left_columns(xl)
    pl.semaphore_wait(barrier, len(partners))
    core = {(0, o): swap_pair(0, o) for o in order}
    zq.start(1, 0)
    xq = send(q_split.at[1 - xl], q_full.at[xl, z], k.at(dxl=1))
    xt = send(l_split.at[1 - xl], l_rows.at[xl], k.at(dxl=1))
    l_copies = left_send(xl)
    y_copies = {}

    def core_sum(q):
        for o in order:
            load_own[q, o].wait()
            core[q, o].wait_recv()
            yy = lax.rem(y + o, 4)

            @pl.loop(0, 8)
            def _(i):
                at = (q, pl.ds(i * 4, 4), pl.ds(yy * 2, 2))
                total = (own[at].astype(F32) + other[at].astype(F32)).astype(BF16)
                for e in range(2):
                    summed[q, yy, e, pl.ds(i * 4, 4)] = total[:, e]

            if o == 2:
                y_copies[q, "far", 1] = send(summed.at[q, yy, 0], y_relay.at[q, 0], k.at(dy=1))
                y_copies[q, "far", 3] = send(summed.at[q, yy, 1], y_relay.at[q, 1], k.at(dy=3))
            elif o:
                e = 1 if o == 1 else 0
                y_copies[q, "near", o] = send(
                    summed.at[q, yy, e], y_recv.at[q, o // 2, e], k.at(dy=o)
                )

    def y_pass(q):
        for e, o in ((0, 1), (1, 3)):
            y_copies[q, "far", o].wait_recv()
            yy = lax.rem(y + o, 4)

            @pl.loop(0, 4)
            def _(i):
                at = pl.ds(i * 8, 8)
                total = summed[q, yy, e, at].astype(F32) + y_relay[q, e, at].astype(F32)
                y_relay[q, e, at] = total.astype(BF16)

            y_copies[q, "sum", o] = send(y_relay.at[q, e], y_recv.at[q, o // 2, e], k.at(dy=o))

    x_copies = {}

    def y_sum(q):
        for o in (1, 3):
            y_copies[q, "near", o].wait_recv()
            y_copies[q, "sum", o].wait_recv()
        for e in range(2):

            @pl.loop(0, 4)
            def _(i):
                at = pl.ds(i * 8, 8)
                total = summed[q, y, e, at].astype(F32)
                for o in range(2):
                    total += y_recv[q, o, e, at].astype(F32)
                acc[pl.ds(e * 512 + i * 128, 128), :] = total.reshape(128, 128)

            for b in range(2):
                for t in range(8):
                    x_send[q, e, b, :, pl.ds(t * 128, 128)] = acc[
                        pl.ds(e * 512 + t * 2 + b, 32, stride=16), :
                    ].astype(BF16)
        for n, (dh, dl) in enumerate(((1, 1), (1, 0), (0, 1))):
            x_copies[q, n] = send(
                x_send.at[q, lax.rem(xh + dh, 2), lax.rem(xl + dl, 2)],
                x_recv.at[q, n],
                k.at(dxh=dh, dxl=dl),
            )

    def x_sum(q):
        at = pl.ds(q * 32, 32)
        x_copies[q, 1].wait_recv()
        g_full[xl, z, at] = (
            x_send[q, xh, xl].astype(F32) + x_recv[q, 1].astype(F32)
        ).astype(BF16)
        zg[q].start(1, 0)
        x_copies[q, 0].wait_recv()
        x_copies[q, 2].wait_recv()
        g_full[1 - xl, z, at] = (x_recv[q, 0].astype(F32) + x_recv[q, 2].astype(F32)).astype(BF16)
        zg[q].start(1, 1)

    def moments_split():
        for n in range(2):
            load_m[n].wait()
            for b in range(2):
                for t in range(8):
                    mom[n, b, :, pl.ds(t * 128, 128)] = mom_in[
                        n, pl.ds(t * 2 + b, 64, stride=16), :
                    ]
        return send(mom.at[:, 1 - xl], mom_recv, k.at(dxl=1))

    core_sum(0)
    core.update({(1, o): swap_pair(1, o) for o in order})
    xq.wait_recv()
    zq.start(1, 1)
    zq.step(1, 0)
    y_pass(0)
    core_sum(1)
    xt.wait_recv()
    left_columns(1 - xl)
    zq.step(1, 1)
    y_sum(0)
    zq.step(2, 0)
    y_pass(1)
    zq.step(2, 1)
    x_sum(0)
    zq.step(3, 0)
    y_sum(1)
    zq.step(3, 1)
    zg[0].steps(1)
    x_sum(1)
    xm = moments_split()
    zg[0].steps(2)
    zg[1].steps(1)
    zg[0].steps(3)
    zg[1].steps(2)
    zg[0].steps(4)
    zg[1].steps(3)
    zq.steps(4)
    zg[1].steps(4)

    def dot(a, b):
        return jnp.dot(a, b, preferred_element_type=F32)

    left = l_rows[...].reshape(128, 1024)
    for t in range(4):
        cols = pl.ds(t * 256, 256)
        y_rot[:, cols] = dot(left, g_full[:, :, :, cols].reshape(1024, 256)).astype(BF16)
    xm.wait_recv()
    for t in range(4):
        cols = pl.ds(t * 256, 256)
        r = dot(y_rot[...], q_full[:, :, :, cols].reshape(1024, 256)).reshape(2, 64, 256)
        r_buf[:, :, cols] = r
        for j in range(2):
            first = mom[0, xl, :, cols] if j == 0 else mom_recv[0, :, cols]
            second = mom[1, xl, :, cols] if j == 0 else mom_recv[1, :, cols]
            rj = r_buf[lax.rem(xl + j, 2), :, cols]
            first = 0.9 * first + 0.1 * rj
            second = 0.95 * second + 0.05 * rj * rj
            n_buf[lax.rem(xl + j, 2), :, cols] = (first / (jnp.sqrt(second) + 1e-8)).astype(BF16)
    normal = n_buf[...].reshape(128, 1024)
    for h in range(H):
        slabs = q_full[...].reshape(1024, 1024)[h * W : (h + 1) * W]
        part = lax.dot_general(normal, slabs, CONTRACT_LAST, preferred_element_type=F32)
        part = part.astype(BF16).reshape(2, 64, W)
        for j in range(2):
            m_full[h, j, z] = part[j]
        if h < 2:
            zm[h].start(1, 0)
            zm[h].start(1, 1)

    l_copies += left_send(1 - xl)
    ret[0] = r_buf[1 - xl].astype(BF16)
    xr = send(ret.at[0], r_recv, k.at(dxl=1))

    def left_gram():
        rows = g_full[:, z].reshape(128, 1024)
        for t in range(4):
            slabs = g_full[...].reshape(1024, 1024)[t * 256 : (t + 1) * 256]
            part = lax.dot_general(rows, slabs, CONTRACT_LAST, preferred_element_type=F32)
            pl_buf[:, :, pl.ds(t * 256, 256)] = part.reshape(2, 64, 256)

    def right_gram():
        half = lax.div(z, 2)
        odd = lax.rem(z, 2) == 1
        wide = lax.broadcasted_iota(jnp.int32, (128, 128), 1) < 64

        for j in range(2):
            for n in range(4):
                at = pl.ds(n * 2, 2)
                a = g_full[j, at, :, pl.ds(pl.multiple_of(half * 128, 128), 128)]
                b = g_full[j, at, :, pl.ds(pl.multiple_of((half + 4) * 128, 128), 128)]
                a, b = a.reshape(128, 128).astype(F32), b.reshape(128, 128).astype(F32)
                a = jnp.where(odd, pltpu.roll(a, 64, 1), a)
                b = jnp.where(odd, b, pltpu.roll(b, 64, 1))
                g_cols[:, pl.ds((j * 4 + n) * 128, 128)] = jnp.where(wide, a, b).T.astype(BF16)
        cols = g_cols[...]
        for t in range(4):
            at = pl.ds(t * 256, 256)
            pr_buf[:, :, at] = dot(cols, g_full[:, :, :, at].reshape(1024, 256)).reshape(2, 64, 256)

    up_copies = {}
    left_t = l_t

    def update(h):
        for t in range(W // 256):
            cols = pl.ds(t * 256, 256)
            part = dot(left_t[...], m_full[h, :, :, :, cols].reshape(1024, 256))
            up_send[h, :, :, cols] = part.astype(BF16).reshape(2, 64, 256)
        up_copies[h] = send(up_send.at[h, 1 - xl], up_recv.at[h], k.at(dxl=1))

    gathers = []

    class Gather:
        def __init__(self, h):
            self.h, self.got = h, {}

        def place(self, dy, dxh, dc, half=None):
            yy, hh, cc = lax.rem(y + dy, 4), lax.rem(xh + dxh, 2), lax.rem(c + dc, 2)
            ref = out.at[(yy * 2 + hh) * 2 + cc, self.h]
            if half is not None:
                ref = ref.at[pl.ds(half * (PIECE // 2), PIECE // 2)]
            return ref

        def push(self, name, src, peer, half=None):
            dst = src
            if src is None:
                src, dst = up_piece.at[self.h], self.place(0, 0, 0)
            self.got[name] = send(src, dst, peer)

        def begin(self):
            self.keep = local(up_piece.at[self.h], self.place(0, 0, 0))
            self.push("x", None, k.at(dxh=1))
            self.push((0, 1), None, k.at(dy=1))
            self.push((0, 3), None, k.at(dy=3))
            self.push((0, 0, "c"), None, k.at(dc=1))

        def x_arrive(self):
            self.got["x"].wait_recv()
            at = self.place(0, 1, 0)
            self.push((1, 1), at, k.at(dy=1))
            self.push((1, 3), at, k.at(dy=3))
            self.push((1, 0, "c"), at, k.at(dc=1))

        def relay(self, e):
            self.got[e, 1].wait_recv()
            self.push((e, 2, 0), self.place(3, e, 0, 0), k.at(dy=1))
            self.got[e, 3].wait_recv()
            self.push((e, 2, 1), self.place(1, e, 0, 1), k.at(dy=3))
            self.push((e, 1, "c"), self.place(3, e, 0), k.at(dc=1))
            self.push((e, 3, "c"), self.place(1, e, 0), k.at(dc=1))

        def finish(self, e):
            self.got[e, 2, 0].wait_recv()
            self.got[e, 2, 1].wait_recv()
            self.push((e, 2, "c"), self.place(2, e, 0), k.at(dc=1))

        def end(self):
            for e in range(2):
                for o in range(4):
                    self.got[e, o, "c"].wait_recv()
            self.keep.wait()

    class GatherYFirst(Gather):
        def begin(self):
            self.keep = local(up_piece.at[self.h], self.place(0, 0, 0))
            self.push((0, 1), None, k.at(dy=1))
            self.push((0, 3), None, k.at(dy=3))
            self.push((0, "x"), None, k.at(dxh=1))
            self.push((0, 0, "c"), None, k.at(dc=1))

        def relay(self, e):
            for o, half in ((1, 0), (3, 1)):
                self.got[0, o].wait_recv()
                self.push((0, 2, half), self.place(4 - o, 0, 0, half), k.at(dy=o))
                self.push((o, "x"), self.place(4 - o, 0, 0), k.at(dxh=1))
                self.push((0, o, "c"), self.place(4 - o, 0, 0), k.at(dc=1))

        def finish(self, e):
            for half in range(2):
                self.got[0, 2, half].wait_recv()
            self.push((2, "x"), self.place(2, 0, 0), k.at(dxh=1))
            self.push((0, 2, "c"), self.place(2, 0, 0), k.at(dc=1))

        def x_arrive(self, steps):
            for o in steps:
                self.got[o, "x"].wait_recv()
                self.push((1, o, "c"), self.place(4 - o if o else 0, 1, 0), k.at(dc=1))

    gathers = [GatherYFirst(0)] + [Gather(h) for h in range(1, H)]

    def pack_up(h):
        up_copies[h].wait_recv()
        n = W // 128
        for b in range(2):
            for t in range(n):
                cols = pl.ds(t * 128, 128)
                mine, theirs = up_send[h, xl, :, cols], up_recv[h, :, cols]
                piece = jnp.where(xl == b, mine.astype(F32), theirs.astype(F32))
                pack[pl.ds(t * 2 + b, 64, stride=2 * n), :] = piece
        up_piece[h] = pack[...].astype(BF16)
        gathers[h].begin()

    def woven(buf, received, b, t):
        cols = pl.ds(t * 128, 128)
        return jnp.where(xl == b, buf[xl, :, cols], received[:, cols].astype(F32))

    def new_moments():
        for b in range(2):
            for t in range(8):
                at = pl.ds(t * 2 + b, 64, stride=16)
                r = woven(r_buf, r_recv, b, t)
                new_first[at, :] = 0.9 * mom_in[0, at, :] + 0.1 * r
                new_second[at, :] = 0.95 * mom_in[1, at, :] + 0.05 * r * r

    def new_gram(dst, n, buf, received):
        load_g[n].wait()
        for b in range(2):
            for t in range(8):
                at = pl.ds(t * 2 + b, 64, stride=16)
                dst[at, :] = 0.95 * gram_in[n, at, :] + 0.05 * woven(buf, received, b, t)

    left_gram()
    ret[1] = pl_buf[1 - xl].astype(BF16)
    xl_copy = send(ret.at[1], pl_recv, k.at(dxl=1))
    zm[0].steps(1)
    zm[2].start(1, 0)
    zm[2].start(1, 1)
    zm[1].steps(1)
    zm[3].start(1, 0)
    zm[3].start(1, 1)
    right_gram()
    ret[2] = pr_buf[1 - xl].astype(BF16)
    xr_copy = send(ret.at[2], pr_recv, k.at(dxl=1))
    zm[0].steps(2)
    zm[2].steps(1)
    zm[1].steps(2)
    zm[3].steps(1)
    for copy in l_copies:
        copy.wait_recv()
    l_t[...] = l_all[...].reshape(1024, 128).astype(F32).T.astype(BF16)
    zm[0].steps(3)
    zm[2].steps(2)
    zm[1].steps(3)
    zm[3].steps(2)
    zm[0].steps(4)
    update(0)
    zm[2].steps(3)
    zm[1].steps(4)
    update(1)
    pack_up(0)
    zm[3].steps(3)
    zm[2].steps(4)
    update(2)
    pack_up(1)
    zm[3].steps(4)
    update(3)
    gathers[0].relay(0)
    pack_up(2)
    gathers[1].x_arrive()
    gathers[1].relay(0)
    pack_up(3)
    xr.wait_recv()
    new_moments()
    results = [local(new_first, new_first_out), local(new_second, new_second_out)]
    gathers[0].finish(0)
    gathers[0].x_arrive((0,))
    gathers[2].x_arrive()
    gathers[2].relay(0)
    gathers[1].finish(0)
    gathers[1].relay(1)
    gathers[3].x_arrive()
    gathers[3].relay(0)
    gathers[0].x_arrive((1, 3))
    xl_copy.wait_recv()
    new_gram(new_left, 0, pl_buf, pl_recv)
    results.append(local(new_left, new_left_out))
    gathers[2].finish(0)
    gathers[2].relay(1)
    gathers[1].finish(1)
    gathers[0].x_arrive((2,))
    xr_copy.wait_recv()
    new_gram(new_right, 1, pr_buf, pr_recv)
    results.append(local(new_right, new_right_out))
    gathers[3].finish(0)
    gathers[3].relay(1)
    gathers[2].finish(1)
    gathers[3].finish(1)
    for gather in gathers:
        gather.end()
    for copy in results:
        copy.wait()
    for copy in unsent:
        copy.wait_send()


def write_out(part, n1, n2, nl, nr, update, o1, o2, ol, orr, held, whole, rest, sems):
    loads, copies = [], []
    top = lax.broadcasted_iota(jnp.int32, (8, 8, 128), 1) < 4
    for n in range(4):
        at = pl.ds(n * 4, 4)
        loads.append(pltpu.make_async_copy(part.at[at], held.at[at], sems.at[n]))
        loads[-1].start()
    for n, src in enumerate((n1, n2, nl, nr)):
        loads.append(pltpu.make_async_copy(src, rest.at[n], sems.at[4 + n]))
        loads[-1].start()
    for n in range(4):
        loads[n].wait()

        @pl.loop(n * 4, n * 4 + 4)
        def _(d):
            for r in range(4):
                a0, a1, a2, a3 = (
                    held[d, h, pl.ds(r * 64, 64), :].astype(F32).reshape(8, 8, 128)
                    for h in range(H)
                )
                even, odd = [], []
                for p, q in ((a0, a1), (a2, a3)):
                    even.append(jnp.where(top, p, pltpu.roll(q, 4, 1)))
                    odd.append(jnp.where(top, pltpu.roll(p, 4, 1), q))
                rows = jnp.stack([jnp.concatenate(even, axis=1), jnp.concatenate(odd, axis=1)], axis=1)
                whole[pl.ds(r * 16, 16), d] = rows.reshape(16, 16, 128).astype(BF16)

        at = (slice(None), pl.ds(n * 4, 4))
        copies.append(pltpu.make_async_copy(whole.at[at], update.at[at], sems.at[8 + n]))
        copies[-1].start()
    for n, dst in enumerate((o1, o2, ol, orr)):
        loads[4 + n].wait()
        copies.append(pltpu.make_async_copy(rest.at[n], dst, sems.at[n]))
        copies[-1].start()
    for copy in copies:
        copy.wait()


def per_device(grads, left_basis_t, right_basis, first, second, left_gram, right_gram):
    g = rows_view(grads[0]).reshape(64, 8, 2, 16, 128)
    lt, qr = (rows_view(a).reshape(64, 16, 128) for a in (left_basis_t, right_basis))
    m1, m2, lg, rg = (rows_view(a).reshape(1024, 128) for a in (first, second, left_gram, right_gram))
    hbm = pl.BlockSpec(memory_space=pl.ANY)
    shape = jax.ShapeDtypeStruct
    v = pltpu.VMEM
    done = pl.pallas_call(
        kernel,
        out_shape=[shape((16, H, PIECE, 128), BF16)] + [shape((1024, 128), F32)] * 4,
        in_specs=[hbm] * 7,
        out_specs=[hbm] * 5,
        scratch_shapes=[
            v((1024, 128), F32),
            v((1024, 128), F32),
            v((1024, 128), F32),
            v((1024, 128), F32),
            v((2, 1024, 128), F32),
            v((2, 64, 16, 128), BF16),
            v((2, 1024, 128), F32),
            v((2, 32, 8, 16, 128), BF16),
            v((2, 32, 8, 16, 128), BF16),
            v((2, 4, 2, 32, 16, 128), BF16),
            v((2, 2, 2, 32, 16, 128), BF16),
            v((2, 2, 32, 16, 128), BF16),
            v((2, 2, 2, 32, 1024), BF16),
            v((2, 3, 32, 1024), BF16),
            v((1024, 128), F32),
            v((2, 64, 1024), BF16),
            v((2, 8, 64, 1024), BF16),
            v((2, 64, 1024), BF16),
            v((2, 64, 1024), BF16),
            v((8, 2, 64, 128), BF16),
            v((2, 8, 64, 128), BF16),
            v((128, 1024), BF16),
            v((2, 8, 64, 1024), BF16),
            v((2, 2, 64, 1024), F32),
            v((2, 64, 1024), F32),
            v((128, 1024), BF16),
            v((2, 64, 1024), BF16),
            v((H, 2, 8, 64, W), BF16),
            v((2, 64, 1024), F32),
            v((64, 1024), BF16),
            v((2, 64, 1024), F32),
            v((64, 1024), BF16),
            v((2, 64, 1024), F32),
            v((64, 1024), BF16),
            v((3, 64, 1024), BF16),
            v((128, 1024), BF16),
            v((H, 2, 64, W), BF16),
            v((H, 64, W), BF16),
            v((PIECE, 128), F32),
            v((H, PIECE, 128), BF16),
            pltpu.SemaphoreType.DMA((NCOPY,)),
            pltpu.SemaphoreType.DMA((NCOPY,)),
            pltpu.SemaphoreType.DMA((24,)),
        ],
        compiler_params=pltpu.CompilerParams(
            collective_id=0, has_side_effects=True, vmem_limit_bytes=56 << 20
        ),
        name="soap",
    )(g, lt, qr, m1, m2, lg, rg)
    update, *rest = pl.pallas_call(
        write_out,
        out_shape=[shape((64, 16, 16, 128), BF16)] + [shape((1024, 128), F32)] * 4,
        in_specs=[hbm] * 5,
        out_specs=[hbm] * 5,
        scratch_shapes=[
            v((16, H, PIECE, 128), BF16),
            v((64, 16, 16, 128), BF16),
            v((4, 1024, 128), F32),
            pltpu.SemaphoreType.DMA((12,)),
        ],
        compiler_params=pltpu.CompilerParams(vmem_limit_bytes=56 << 20),
        name="write_out",
    )(*done)
    update = update.reshape(64, 128, 2, 128).transpose(0, 2, 1, 3).reshape(64, 2, 16384)

    def back(a):
        return a.reshape(64, 8, 2, 128).transpose(0, 2, 1, 3).reshape(64, 2, 1024)

    return (update, *(back(a) for a in rest))


def solution(mesh):
    sharded = P("fsdp", None, "dp")
    return jax.shard_map(
        per_device,
        mesh=mesh,
        in_specs=(P("dp", "fsdp", None, None),) + (sharded,) * 6,
        out_specs=(P("fsdp", None, None),) + (sharded,) * 4,
        check_vma=False,
    )
```
